128 devices in a mesh: seq: 64 (over x, y, z_hi, core), head: 2 (over z_lo).
Axes of the slice: x: 4, y: 4, z: 4 (z_hi: 2, z_lo: 2; z = z_hi * 2 + z_lo), core: 2. Of those that a mesh axis runs over, the one named last changes fastest.
Arguments:
- queries: bfloat16 [8, 32768, 128], P('head', 'seq'), may hold values from -6 to 6
- key_rows: bfloat16 [32768, 128], P('seq'), may hold values from -6 to 6
- value_rows: bfloat16 [32768, 128], P('seq'), may hold values from -6 to 6
- d_out: bfloat16 [8, 32768, 128], P('head', 'seq'), may hold values from -6 to 6
- seq_lengths: int32 [16], replicated, may hold values from 1 to 4096, 32768 in all
Outputs:
- attended: bfloat16 [8, 32768, 128], P('head', 'seq')
- grad_queries: bfloat16 [8, 32768, 128], P('head', 'seq')
- grad_keys: bfloat16 [32768, 128], P('seq')
- grad_values: bfloat16 [32768, 128], P('seq')
The draws below stay inside these ranges and needn't reach their ends.
All inputs are finite; a program needn't handle non-finite values.
Results may differ from the reference program's by a relative error of at most 0.034.
Values may be sent and summed in bfloat16 or wider, within the bound.
No kernel may reach another device: no remote copies, remote signals or barrier semaphores. Data moves between devices by JAX's collectives and lax.ppermute only.
A program may use at most 128 MiB of HBM per device.

```python
import math
import jax
import jax.numpy as jnp
import numpy as np
from jax import lax

HD = 128
HQ = 8
TOK_DEV = 512
SPAN = 8
TOKENS = 32768
MOST = 4096
DOCS = 16


def draw_queries(key, part):
    key = jax.random.fold_in(key, 1)
    sample = jax.random.truncated_normal(key, -6.0, 6.0, (HQ, TOKENS, HD), jnp.float32)
    return sample.astype(jnp.bfloat16)


def draw_key_rows(key, part):
    key = jax.random.fold_in(key, 2)
    sample = jax.random.truncated_normal(key, -6.0, 6.0, (TOKENS, HD), jnp.float32)
    return sample.astype(jnp.bfloat16)


def shard_levels(own_key, dims, cuts, low, largest):
    def one(position, parts):
        heights = jax.random.uniform(jax.random.fold_in(jax.random.fold_in(own_key, 6), position), (parts,), jnp.float32, low / len(cuts), largest / len(cuts))
        return jnp.repeat(jnp.exp(heights), dims[position] // parts).reshape((-1,) + (1,) * (len(dims) - position - 1))

    factor_of = one(*cuts[0])
    for cut in cuts[1:]:
        factor_of = factor_of * one(*cut)
    return factor_of


def profile(amount, total, reach, lean):
    weights = [(1 << 20) // math.isqrt(rank ** lean) + 1 for rank in range(2, amount + 1)]
    surplus, given = total - reach - (amount - 1), [1] * (amount - 1)
    while surplus > 0:
        candidates = [i for i in range(amount - 1) if given[i] < reach]
        pool, left = sum([weights[i] for i in candidates]), surplus
        for i in candidates:
            extra = min(reach - given[i], max(1, left * weights[i] // pool), surplus)
            given[i] = given[i] + extra
            surplus = surplus - extra
    return np.array([reach] + given)


def ragged_sizes(rng, number_of, total, bound, skew):
    if number_of == 2:
        one = jax.random.randint(rng, (), max(1, total - bound), min(bound, total - 1) + 1)
        return jnp.stack([one, total - one])
    tallies = jnp.asarray(profile(number_of, total, bound, skew), jnp.int32)
    twos = (number_of - 1) // 2
    donor, receiver = tallies[1:1 + 2 * twos:2], tallies[2:2 + 2 * twos:2]
    room = jnp.minimum(donor - 1, bound - receiver)
    shifted = jax.random.randint(jax.random.fold_in(rng, 1), (twos,), 0, 1 << 20) % (room + 1)
    tallies = tallies.at[1:1 + 2 * twos:2].set(donor - shifted).at[2:2 + 2 * twos:2].set(receiver + shifted)
    return tallies[jax.random.permutation(jax.random.fold_in(rng, 2), number_of)]


def gaussian(key, shape, width, most, cuts=(), held_as=jnp.bfloat16):
    values = jax.random.normal(key, shape, jnp.float32) * width
    if len(cuts) > 0:
        values = shard_levels(key, shape, cuts, -0.22, 0.18) * values
    return jnp.clip(values, min=-most, max=most).astype(held_as)


def setup_inputs(seed: int = 0) -> dict:
    splits = jax.random.split(jax.random.key(seed), 6)
    queries = draw_queries(jax.random.fold_in(splits[5], 71), 0)
    key_rows = draw_key_rows(jax.random.fold_in(splits[5], 71), 0)
    value_rows = gaussian(splits[2], (TOKENS, HD), 1.0, 6.0, ((0, 64),))
    d_out = gaussian(splits[3], (HQ, TOKENS, HD), 1.0, 6.0, ((0, 2), (1, 64)))
    seq_lengths = ragged_sizes(splits[4], DOCS, TOKENS, MOST, 2).astype(jnp.int32)
    return {"queries": queries, "key_rows": key_rows, "value_rows": value_rows, "d_out": d_out, "seq_lengths": seq_lengths}


def segment_of(positions, seq_lengths):
    seq_ends = jnp.cumsum(seq_lengths).astype(jnp.int32)
    return jnp.sum((positions[:, None] >= seq_ends[None, :]).astype(jnp.int32), axis=1).astype(jnp.int32)


def reference(queries, key_rows, value_rows, d_out, seq_lengths):
    head_count, tokens, head_size = queries.shape
    row_count = TOK_DEV
    blocks = tokens // row_count
    margin = SPAN * row_count
    window = margin + row_count
    scaling = head_size ** -0.5
    key_pos = jnp.arange(-margin, tokens, dtype=jnp.int32)
    key_seg = jnp.where(key_pos >= 0, segment_of(key_pos, seq_lengths), -1).astype(jnp.int32)
    padding = jnp.zeros((margin, head_size), jnp.float32)
    key_all = jnp.concatenate([padding, key_rows.astype(jnp.float32)], 0)
    value_all = jnp.concatenate([padding, value_rows.astype(jnp.float32)], 0)
    query_all = queries.astype(jnp.float32)
    grad_all = d_out.astype(jnp.float32)

    def pieces(block):
        first_row = (block * row_count).astype(jnp.int32)
        query_block = lax.dynamic_slice_in_dim(query_all, first_row, row_count, 1)
        key_window = lax.dynamic_slice_in_dim(key_all, first_row, window, 0)
        value_window = lax.dynamic_slice_in_dim(value_all, first_row, window, 0)
        query_pos = first_row + jnp.arange(row_count, dtype=jnp.int32)
        query_seg = segment_of(query_pos, seq_lengths)
        window_pos = lax.dynamic_slice_in_dim(key_pos, first_row, window, 0)
        window_seg = lax.dynamic_slice_in_dim(key_seg, first_row, window, 0)
        allowed = (window_seg[None, :] == query_seg[:, None]) & (window_pos[None, :] <= query_pos[:, None])
        scores = jnp.einsum("hqd,kd->hqk", query_block, key_window) * scaling
        return first_row, query_block, key_window, value_window, allowed, scores

    def forward(block):
        first_row, query_block, key_window, value_window, allowed, scores = pieces(block)
        scores = jnp.where(allowed[None], scores, -1e30)
        row_max = jnp.max(scores, axis=2)
        weights = jnp.exp(scores - row_max[..., None])
        row_total = jnp.sum(weights, axis=2)
        product = jnp.einsum("hqk,kd->hqd", weights, value_window, precision=lax.Precision.HIGHEST)
        result = (product / row_total[..., None]).astype(jnp.bfloat16)
        return result, row_max + jnp.log(row_total)

    block_ids = jnp.arange(blocks, dtype=jnp.int32)
    outs, lses = lax.map(forward, block_ids)
    attended = jnp.transpose(outs, (1, 0, 2, 3)).reshape(head_count, tokens, head_size)
    lse = jnp.transpose(lses, (1, 0, 2)).reshape(head_count, tokens)
    row_delta = jnp.sum(grad_all * attended.astype(jnp.float32), axis=2)

    def backward(partial_sums, block):
        grad_key_all, grad_value_all = partial_sums
        first_row, query_block, key_window, value_window, allowed, scores = pieces(block)
        grad_block = lax.dynamic_slice_in_dim(grad_all, first_row, row_count, 1)
        lse_block = lax.dynamic_slice_in_dim(lse, first_row, row_count, 1)
        delta_block = lax.dynamic_slice_in_dim(row_delta, first_row, row_count, 1)
        probabilities = jnp.where(allowed[None], jnp.exp(scores - lse_block[..., None]), 0.0)
        rounded = lax.optimization_barrier(probabilities.astype(jnp.bfloat16)).astype(jnp.float32)
        value_grad = jnp.einsum("hqk,hqd->kd", rounded, grad_block)
        dprobs = jnp.einsum("hqd,kd->hqk", grad_block, value_window)
        dscores = (probabilities * (dprobs - delta_block[..., None])).astype(jnp.bfloat16)
        dscores = lax.optimization_barrier(dscores).astype(jnp.float32)
        query_grad = (jnp.einsum("hqk,kd->hqd", dscores, key_window) * scaling).astype(jnp.bfloat16)
        key_grad = jnp.einsum("hqk,hqd->kd", dscores, query_block) * scaling
        old_key = lax.dynamic_slice_in_dim(grad_key_all, first_row, window, 0)
        old_value = lax.dynamic_slice_in_dim(grad_value_all, first_row, window, 0)
        grad_key_all = lax.dynamic_update_slice_in_dim(grad_key_all, old_key + key_grad, first_row, 0)
        grad_value_all = lax.dynamic_update_slice_in_dim(grad_value_all, old_value + value_grad, first_row, 0)
        return (grad_key_all, grad_value_all), query_grad

    zeros_all = jnp.zeros((margin + tokens, head_size), jnp.float32)
    (grad_key_all, grad_value_all), query_grads = lax.scan(backward, (zeros_all, zeros_all), block_ids)
    grad_queries = jnp.transpose(query_grads, (1, 0, 2, 3)).reshape(head_count, tokens, head_size)
    grad_keys = grad_key_all[margin:].astype(jnp.bfloat16)
    grad_values = grad_value_all[margin:].astype(jnp.bfloat16)
    return attended, grad_queries, grad_keys, grad_values
```

```python
from functools import partial
import math

import jax
import jax.numpy as jnp
from jax import lax
from jax.experimental import pallas as pl
from jax.experimental.pallas import tpu as pltpu
from jax.sharding import Mesh, PartitionSpec as P

NEGATIVE = -1e30
BLK = 512
HEADS = 4
HD = 128
NQ = HEADS * BLK
ROWS = 3
SLOTS = 4 * ROWS
SPAN = 9
SCALE = HD ** -0.5
LOG2 = SCALE * math.log2(math.e)
F32 = jnp.float32
BF16 = jnp.bfloat16
SEQ = ("x", "y", "zh", "core")


def dot(a, b):
    return lax.dot_general(a, b, (((1,), (0,)), ((), ())), preferred_element_type=F32)


def attention_kernel(*refs):
    len_ref, q_ref, do_ref = refs[:3]
    kv_refs = refs[3:15]
    o_ref, dq_ref = refs[15:17]
    out_refs = refs[17:23]
    (kvs, dkvs, qt, dot_t, probs, tile_max, run_max, total, acc, dq_acc, stage_p, stage_s, delta, in_sem, out_sem) = refs[23:]
    row = lax.axis_index("x") * 4 + lax.axis_index("y")
    zh = lax.axis_index("zh")
    core = lax.axis_index("core")
    place = zh * 2 + core

    def slot_of(j, dz, dc):
        return (2 - j) * 4 + (1 - zh if dz else zh) * 2 + (1 - core if dc else core)

    order = [(j, dz, dc) for j in range(ROWS) for dz in range(2) for dc in range(2)]
    copies = []
    for n, (j, dz, dc) in enumerate(order):
        copies.append(pltpu.make_async_copy(kv_refs[n], kvs.at[slot_of(j, dz, dc)], in_sem.at[n]))
        copies[-1].start()

    base = (row - 2) * (4 * BLK)
    first = base + (8 + place) * BLK
    q_pos = lax.broadcasted_iota(jnp.int32, (1, BLK), 1) + (8 + place) * BLK
    starts = jnp.zeros((1, BLK), jnp.int32) - base
    first_start = -base
    last_start = -base
    end = jnp.int32(0)
    for c in range(16):
        end = end + len_ref[c]
        rel = end - base
        starts = jnp.where(q_pos >= rel, rel, starts)
        first_start = jnp.where(end <= first, rel, first_start)
        last_start = jnp.where(end <= first + BLK - 1, rel, last_start)
    lo = first_start // BLK
    hi = 8 + place

    for h in range(HEADS):
        cols = slice(h * BLK, (h + 1) * BLK)
        qt[:, cols] = q_ref[h].T
        dot_t[:, cols] = do_ref[h].T
    run_max[...] = jnp.full((1, NQ), NEGATIVE, F32)
    total[...] = jnp.zeros((1, NQ), F32)
    acc[...] = jnp.zeros((HD, NQ), F32)
    dq_acc[...] = jnp.zeros((HD, NQ), F32)
    for copy in copies:
        copy.wait()

    def forward(t, masked):
        k = kvs[t, 0]
        v_t = kvs[t, 1].T
        if masked:
            k_pos = lax.broadcasted_iota(jnp.int32, (BLK, BLK), 0) + t * BLK
            allowed = (k_pos >= starts) & (k_pos <= q_pos)
        for h in range(HEADS):
            cols = slice(h * BLK, (h + 1) * BLK)
            s = dot(k, qt[:, cols])
            if masked:
                s = jnp.where(allowed, s, NEGATIVE)
            old = run_max[:, cols]
            new = jnp.maximum(old, jnp.max(s, axis=0, keepdims=True))
            p = jnp.exp2((s - new) * LOG2)
            factor = jnp.exp2((old - new) * LOG2)
            total[:, cols] = total[:, cols] * factor + jnp.sum(p, axis=0, keepdims=True)
            run_max[:, cols] = new
            tile_max[t - lo, :, cols] = new
            p = p.astype(BF16)
            probs[t - lo, :, cols] = p
            acc[:, cols] = acc[:, cols] * factor + dot(v_t, p)

    def forward_step(t, carry):
        masked = (t * BLK < last_start) | (t == hi)

        @pl.when(masked)
        def _():
            forward(t, True)

        @pl.when(jnp.logical_not(masked))
        def _():
            forward(t, False)

        return carry

    lax.fori_loop(lo, hi + 1, forward_step, 0)

    total[...] = 1.0 / total[...]
    for h in range(HEADS):
        cols = slice(h * BLK, (h + 1) * BLK)
        o = (acc[:, cols] * total[:, cols]).astype(BF16)
        o_ref[h] = o.T
        delta[:, cols] = jnp.sum(o.astype(F32) * dot_t[:, cols].astype(F32), axis=0, keepdims=True)

    def backward_step(t, carry):
        k_t = kvs[t, 0].T
        v = kvs[t, 1]
        for h in range(HEADS):
            cols = slice(h * BLK, (h + 1) * BLK)
            factor = jnp.exp2((tile_max[t - lo, :, cols] - run_max[:, cols]) * LOG2) * total[:, cols]
            p = probs[t - lo, :, cols].astype(F32) * factor
            stage_p[:, cols] = p.astype(BF16)
            dp = dot(v, dot_t[:, cols])
            ds = (p * (dp - delta[:, cols])).astype(BF16)
            stage_s[:, cols] = ds
            dq_acc[:, cols] += dot(k_t, ds)
        dkvs[t, 1] = dot(stage_p[...], do_ref[...].reshape(NQ, HD)).astype(BF16)
        dkvs[t, 0] = (dot(stage_s[...], q_ref[...].reshape(NQ, HD)) * SCALE).astype(BF16)
        return carry

    lax.fori_loop(lo, hi + 1, backward_step, 0)

    def clear(t, carry):
        dkvs[t] = jnp.zeros((2, BLK, HD), BF16)
        return carry

    lax.fori_loop(0, lo, clear, 0)
    lax.fori_loop(hi + 1, SLOTS, clear, 0)
    copies = []
    for n, (j, dz, dc) in enumerate(order):
        copies.append(pltpu.make_async_copy(dkvs.at[slot_of(j, dz, dc)], out_refs[j * 2 + dc].at[dz], out_sem.at[n]))
        copies[-1].start()
    for h in range(HEADS):
        cols = slice(h * BLK, (h + 1) * BLK)
        dq_ref[h] = (dq_acc[:, cols] * SCALE).astype(BF16).T
    for copy in copies:
        copy.wait()


def attention(seq_lengths, queries, d_out, blocks):
    vmem = pl.BlockSpec(memory_space=pltpu.VMEM)
    anywhere = pl.BlockSpec(memory_space=pl.ANY)
    pair = jax.ShapeDtypeStruct((2, 2, BLK, HD), BF16)
    rows = jax.ShapeDtypeStruct((HEADS, BLK, HD), BF16)
    return pl.pallas_call(
        attention_kernel,
        out_shape=(rows, rows) + (pair,) * 6,
        in_specs=[pl.BlockSpec(memory_space=pltpu.SMEM), vmem, vmem] + [anywhere] * 12,
        out_specs=[vmem, vmem] + [anywhere] * 6,
        scratch_shapes=[
            pltpu.VMEM((SLOTS, 2, BLK, HD), BF16),
            pltpu.VMEM((SLOTS, 2, BLK, HD), BF16),
            pltpu.VMEM((HD, NQ), BF16),
            pltpu.VMEM((HD, NQ), BF16),
            pltpu.VMEM((SPAN, BLK, NQ), BF16),
            pltpu.VMEM((SPAN, 1, NQ), F32),
            pltpu.VMEM((1, NQ), F32),
            pltpu.VMEM((1, NQ), F32),
            pltpu.VMEM((HD, NQ), F32),
            pltpu.VMEM((HD, NQ), F32),
            pltpu.VMEM((BLK, NQ), BF16),
            pltpu.VMEM((BLK, NQ), BF16),
            pltpu.VMEM((1, NQ), F32),
            pltpu.SemaphoreType.DMA((SLOTS,)),
            pltpu.SemaphoreType.DMA((SLOTS,)),
        ],
        compiler_params=pltpu.CompilerParams(vmem_limit_bytes=56 << 20),
        cost_estimate=pl.CostEstimate(flops=8 << 30, bytes_accessed=16 << 20, transcendentals=9 << 20),
        name="attention",
    )(seq_lengths, queries, d_out, *blocks)


def swap_core(value):
    return lax.ppermute(value, "core", [(0, 1), (1, 0)])


def swap_z(value):
    return lax.ppermute(value, ("zh", "zl"), [(0, 3), (3, 0), (1, 2), (2, 1)])


def swap_head(value):
    return lax.ppermute(value, "zl", [(0, 1), (1, 0)])


def shift_row(value, by):
    return lax.ppermute(value, ("x", "y"), [(r, (r + by) % 16) for r in range(16)])


def added(a, b):
    return (a.astype(F32) + b.astype(F32)).astype(BF16)


def on_device(queries, key_rows, value_rows, d_out, seq_lengths):
    own = jnp.stack([key_rows, value_rows])
    row1 = shift_row(own, 1)
    side0 = swap_z(own)
    row2 = shift_row(row1, 1)
    side1 = swap_z(row1)
    side2 = swap_z(row2)
    mine = [own, side0, row1, side1, row2, side2]
    blocks = []
    for block in mine:
        blocks += [block, swap_core(block)]
    attended, grad_queries, *parts = attention(seq_lengths, queries, d_out, blocks)

    def column(j):
        keep, send = parts[2 * j], parts[2 * j + 1]
        both = added(keep, swap_core(send))
        return added(both[0], swap_z(both[1]))

    back = shift_row(column(2), -1)
    back = shift_row(added(column(1), back), -1)
    half = added(column(0), back)
    other = swap_head(half)
    grads = half.astype(F32) + other.astype(F32)
    grads = grads.astype(BF16)
    return attended, grad_queries, grads[0], grads[1]


def solution(mesh):
    fine = Mesh(mesh.devices.reshape(4, 4, 2, 2, 2), ("x", "y", "zh", "core", "zl"))
    tokens = P("zl", SEQ, None)
    rows = P(SEQ, None)
    return jax.shard_map(
        on_device,
        mesh=fine,
        in_specs=(tokens, rows, rows, tokens, P()),
        out_specs=(tokens, tokens, rows, rows),
        check_vma=False,
    )
```

```python
from functools import partial
import math

import jax
import jax.numpy as jnp
from jax import lax
from jax.experimental import pallas as pl
from jax.experimental.pallas import tpu as pltpu
from jax.sharding import Mesh, PartitionSpec as P

NEGATIVE = -1e30
BLK = 512
HEADS = 4
HD = 128
NQ = HEADS * BLK
HALF = BLK // 2
ROWS = 3
SLOTS = 4 * ROWS
SPAN = 9
SCALE = HD ** -0.5
LOG2 = SCALE * math.log2(math.e)
BOUND = 64.0
F32 = jnp.float32
BF16 = jnp.bfloat16
SEQ = ("x", "y", "zh", "core")


def dot(a, b):
    return lax.dot_general(a, b, (((1,), (0,)), ((), ())), preferred_element_type=F32)


def attention_kernel(*refs):
    len_ref, q_ref, do_ref = refs[:3]
    kv_refs = refs[3:27]
    o_ref, dq_ref = refs[27:29]
    out_refs = refs[29:35]
    (kvs, dkvs, qt, dot_t, do_s, probs, row_max, total, acc, dq_acc, stage_s, delta, in_sem, out_sem) = refs[35:]
    row = lax.axis_index("x") * 4 + lax.axis_index("y")
    zh = lax.axis_index("zh")
    core = lax.axis_index("core")
    zl = lax.axis_index("zl")
    place = zh * 2 + core

    def slot_of(j, dz, dc):
        return (2 - j) * 4 + (1 - zh if dz else zh) * 2 + (1 - core if dc else core)

    def part_of(dp):
        return 1 - zl if dp else zl

    order = [(j, dz, dp, dc) for j in range(ROWS) for dz in range(2) for dp in range(2) for dc in range(2)]

    def in_copy(n):
        j, dz, dp, dc = order[n]
        slot = slot_of(j, dz, dc)
        return pltpu.make_async_copy(kv_refs[n], kvs.at[slot, part_of(dp)], in_sem.at[n])

    for n in range(len(order)):
        in_copy(n).start()

    base = (row - 2) * (4 * BLK)
    first = base + (8 + place) * BLK
    q_pos = lax.broadcasted_iota(jnp.int32, (1, BLK), 1) + (8 + place) * BLK
    starts = jnp.zeros((1, BLK), jnp.int32) - base
    first_start = -base
    last_start = -base
    end = jnp.int32(0)
    for c in range(16):
        end = end + len_ref[c]
        rel = end - base
        starts = jnp.where(q_pos >= rel, rel, starts)
        first_start = jnp.where(end <= first, rel, first_start)
        last_start = jnp.where(end <= first + BLK - 1, rel, last_start)
    lo = first_start // BLK
    hi = 8 + place

    for h in range(HEADS):
        cols = slice(h * BLK, (h + 1) * BLK)
        qt[:, cols] = q_ref[h].T
        dot_t[:, cols] = do_ref[h].T
    row_max[...] = jnp.zeros((1, NQ), F32)
    total[...] = jnp.zeros((1, NQ), F32)
    acc[...] = jnp.zeros((HD, NQ), F32)
    dq_acc[...] = jnp.zeros((HD, NQ), F32)
    q_norm = jnp.max(dot(jnp.ones((8, HD), BF16), jnp.square(qt[...].astype(F32)).astype(BF16)))
    for n in range(len(order)):
        in_copy(n).wait()

    def norm_step(t, k_norm):
        norms = dot(jnp.square(kvs[t, 0].astype(F32)).astype(BF16), jnp.ones((HD, HD), BF16))
        return jnp.maximum(k_norm, jnp.max(norms.reshape(BLK // 8, 8, HD), axis=0))

    k_norm = jnp.max(lax.fori_loop(lo, hi + 1, norm_step, jnp.zeros((8, HD), F32)))
    safe = q_norm * k_norm <= 0.98 * (BOUND / LOG2) ** 2

    def tile_mask(t):
        k_pos = lax.broadcasted_iota(jnp.int32, (BLK, BLK), 0) + t * BLK
        return (k_pos >= starts) & (k_pos <= q_pos)

    def max_step(t, carry):
        allowed = tile_mask(t)
        for h in range(HEADS):
            cols = slice(h * BLK, (h + 1) * BLK)
            s = jnp.where(allowed, dot(kvs[t, 0], qt[:, cols]), NEGATIVE)
            row_max[:, cols] = jnp.maximum(row_max[:, cols], jnp.max(s, axis=0, keepdims=True))
        return carry

    @pl.when(jnp.logical_not(safe))
    def _():
        row_max[...] = jnp.full((1, NQ), NEGATIVE, F32)
        lax.fori_loop(lo, hi + 1, max_step, 0)
        row_max[...] = row_max[...] * LOG2

    def forward(t, masked):
        k = kvs[t, 0]
        v_t = kvs[t, 1].T
        if masked:
            allowed = tile_mask(t)
        def score(h):
            s = dot(k, qt[:, h * HALF:(h + 1) * HALF])
            return jnp.where(allowed[:, (h % 2) * HALF:(h % 2 + 1) * HALF], s, NEGATIVE) if masked else s

        def soft(h, s):
            cols = slice(h * HALF, (h + 1) * HALF)
            p = jnp.exp2(s * LOG2 - row_max[:, cols])
            total[:, cols] += jnp.sum(p, axis=0, keepdims=True)
            p = p.astype(BF16)
            probs[t - lo, :, cols] = p
            return p

        def pv(h, p):
            cols = slice(h * HALF, (h + 1) * HALF)
            acc[:, cols] += dot(v_t, p)

        weights = soft(0, score(0))
        s = score(1)
        for h in range(1, 2 * HEADS):
            held, weights = weights, soft(h, s)
            if h + 1 < 2 * HEADS:
                s = score(h + 1)
            pv(h - 1, held)
        pv(2 * HEADS - 1, weights)

    def forward_step(t, carry):
        masked = (t * BLK < last_start) | (t == hi)

        @pl.when(masked)
        def _():
            forward(t, True)

        @pl.when(jnp.logical_not(masked))
        def _():
            forward(t, False)

        return carry

    lax.fori_loop(lo, hi + 1, forward_step, 0)

    for h in range(HEADS):
        cols = slice(h * BLK, (h + 1) * BLK)
        inverse = 1.0 / total[:, cols]
        o = (acc[:, cols] * inverse).astype(BF16)
        o_ref[h] = o.T
        scaled = (dot_t[:, cols].astype(F32) * inverse).astype(BF16)
        dot_t[:, cols] = scaled
        do_s[h * BLK:(h + 1) * BLK] = scaled.T
        delta[:, cols] = jnp.sum(o.astype(F32) * scaled.astype(F32), axis=0, keepdims=True)

    def out_copy(n, t):
        j, dz, dp, dc = order[n]
        return pltpu.make_async_copy(dkvs.at[t, part_of(dp)], out_refs[j * 2 + dc].at[dz, dp], out_sem.at[n])

    def send_out(t):
        for n, (j, dz, dp, dc) in enumerate(order):
            if dp == 0:
                @pl.when(slot_of(j, dz, dc) == t)
                def _():
                    out_copy(n, t).start()
                    out_copy(n + 2, t).start()

    dkvs[SLOTS] = jnp.zeros((2, BLK, HD), BF16)
    for n, (j, dz, dp, dc) in enumerate(order):
        slot = slot_of(j, dz, dc)

        @pl.when((slot < lo) | (slot > hi))
        def _():
            out_copy(n, SLOTS).start()

    def backward_step(t, carry):
        k_t = kvs[t, 0].T
        v = kvs[t, 1]
        def dp_of(h):
            return dot(v, dot_t[:, h * BLK:(h + 1) * BLK])

        def ds_of(h, dp):
            cols = slice(h * BLK, (h + 1) * BLK)
            ds = (probs[t - lo, :, cols].astype(F32) * (dp - delta[:, cols])).astype(BF16)
            stage_s[:, cols] = ds
            return ds

        def dq_of(h, ds):
            dq_acc[:, h * BLK:(h + 1) * BLK] += dot(k_t, ds)

        d0 = dp_of(0)
        d1 = dp_of(1)
        s0 = ds_of(0, d0)
        dkvs[t, 1] = dot(probs[t - lo], do_s[...]).astype(BF16)
        d2 = dp_of(2)
        dq_of(0, s0)
        s1 = ds_of(1, d1)
        d3 = dp_of(3)
        dq_of(1, s1)
        s2 = ds_of(2, d2)
        dq_of(2, s2)
        s3 = ds_of(3, d3)
        dq_of(3, s3)
        dkvs[t, 0] = (dot(stage_s[...], q_ref[...].reshape(NQ, HD)) * SCALE).astype(BF16)
        send_out(t)
        return carry

    lax.fori_loop(lo, hi + 1, backward_step, 0)

    copies = [out_copy(n, 0) for n in range(len(order))]
    for h in range(HEADS):
        cols = slice(h * BLK, (h + 1) * BLK)
        dq_ref[h] = (dq_acc[:, cols] * SCALE).astype(BF16).T
    for copy in copies:
        copy.wait()


def attention(seq_lengths, queries, d_out, blocks):
    vmem = pl.BlockSpec(memory_space=pltpu.VMEM)
    anywhere = pl.BlockSpec(memory_space=pl.ANY)
    pair = jax.ShapeDtypeStruct((2, 2, BLK, HD), BF16)
    rows = jax.ShapeDtypeStruct((HEADS, BLK, HD), BF16)
    return pl.pallas_call(
        attention_kernel,
        out_shape=(rows, rows) + (pair,) * 6,
        in_specs=[pl.BlockSpec(memory_space=pltpu.SMEM), vmem, vmem] + [anywhere] * 24,
        out_specs=[vmem, vmem] + [anywhere] * 6,
        scratch_shapes=[
            pltpu.VMEM((SLOTS, 2, BLK, HD), BF16),
            pltpu.VMEM((SLOTS + 1, 2, BLK, HD), BF16),
            pltpu.VMEM((HD, NQ), BF16),
            pltpu.VMEM((HD, NQ), BF16),
            pltpu.VMEM((NQ, HD), BF16),
            pltpu.VMEM((SPAN, BLK, NQ), BF16),
            pltpu.VMEM((1, NQ), F32),
            pltpu.VMEM((1, NQ), F32),
            pltpu.VMEM((HD, NQ), F32),
            pltpu.VMEM((HD, NQ), F32),
            pltpu.VMEM((BLK, NQ), BF16),
            pltpu.VMEM((1, NQ), F32),
            pltpu.SemaphoreType.DMA((2 * SLOTS,)),
            pltpu.SemaphoreType.DMA((2 * SLOTS,)),
        ],
        compiler_params=pltpu.CompilerParams(vmem_limit_bytes=56 << 20),
        cost_estimate=pl.CostEstimate(flops=8 << 30, bytes_accessed=16 << 20, transcendentals=9 << 20),
        name="attention",
    )(seq_lengths, queries, d_out, *blocks)


def swap_core(value):
    return lax.ppermute(value, "core", [(0, 1), (1, 0)])


def to_column(value, dz, dp, sources=(0, 1)):
    pairs = [(2 * zh + zl, 2 * (zh ^ dz) + (zl ^ dp)) for zh in sources for zl in range(2)]
    return lax.ppermute(value, ("zh", "zl"), pairs)


def shift_row(value, by):
    return lax.ppermute(value, ("x", "y"), [(r, (r + by) % 16) for r in range(16)])


def added(*values):
    total = values[0].astype(F32)
    for value in values[1:]:
        total = total + value.astype(F32)
    return total.astype(BF16)


def on_device(queries, key_rows, value_rows, d_out, seq_lengths):
    zl = lax.axis_index("zl")
    mine = jnp.where(zl == 0, key_rows, value_rows)
    other = jnp.where(zl == 0, value_rows, key_rows)
    row1 = shift_row(mine, 1)
    row2 = shift_row(row1, 1)
    pieces = [
        mine, other, to_column(other, 1, 1, (0,)), to_column(mine, 1, 1, (0,)),
        row1, to_column(row1, 0, 1), to_column(row1, 1, 0), to_column(row1, 1, 1),
        row2, to_column(row2, 0, 1), to_column(row2, 1, 0, (1,)), to_column(row2, 1, 1, (1,)),
    ]
    blocks = []
    for piece in pieces:
        blocks += [piece, swap_core(piece)]
    attended, grad_queries, *parts = attention(seq_lengths, queries, d_out, blocks)

    def column(j, sources):
        both = added(parts[2 * j], swap_core(parts[2 * j + 1]))
        return added(
            both[0, 0],
            to_column(both[0, 1], 0, 1),
            to_column(both[1, 0], 1, 0, sources),
            to_column(both[1, 1], 1, 1, sources),
        )

    back = shift_row(column(2, (0,)), -1)
    back = shift_row(added(column(1, (0, 1)), back), -1)
    done = added(column(0, (1,)), back)
    given = to_column(done, 0, 1)
    grad_keys = jnp.where(zl == 0, done, given)
    grad_values = jnp.where(zl == 0, given, done)
    return attended, grad_queries, grad_keys, grad_values


def solution(mesh):
    fine = Mesh(mesh.devices.reshape(4, 4, 2, 2, 2), ("x", "y", "zh", "core", "zl"))
    tokens = P("zl", SEQ, None)
    rows = P(SEQ, None)
    return jax.shard_map(
        on_device,
        mesh=fine,
        in_specs=(tokens, rows, rows, tokens, P()),
        out_specs=(tokens, tokens, rows, rows),
        check_vma=False,
    )
```

```python
from functools import partial
import math

import jax
import jax.numpy as jnp
from jax import lax
from jax.experimental import pallas as pl
from jax.experimental.pallas import tpu as pltpu
from jax.sharding import Mesh, PartitionSpec as P

NEGATIVE = -1e30
BLK = 512
HEADS = 4
HD = 128
NQ = HEADS * BLK
HALF = BLK // 2
ROWS = 3
SLOTS = 4 * ROWS
SPAN = 9
SCALE = HD ** -0.5
LOG2 = SCALE * math.log2(math.e)
BOUND = 64.0
F32 = jnp.float32
BF16 = jnp.bfloat16
SEQ = ("x", "y", "zh", "core")


def dot(a, b):
    return lax.dot_general(a, b, (((1,), (0,)), ((), ())), preferred_element_type=F32)


def attention_kernel(*refs):
    len_ref, q_ref, do_ref = refs[:3]
    kv_refs = refs[3:27]
    o_ref, dq_ref = refs[27:29]
    out_refs = refs[29:33]
    (kvs, dkvs, qt, dot_t, do_s, probs, row_max, total, acc, dq_acc, stage_s, delta, in_sem, out_sem) = refs[33:]
    row = lax.axis_index("x") * 4 + lax.axis_index("y")
    zh = lax.axis_index("zh")
    core = lax.axis_index("core")
    place = zh * 2 + core

    def slot_of(j, dz, dc):
        return (2 - j) * 4 + (1 - zh if dz else zh) * 2 + (1 - core if dc else core)

    order = [(j, dz, part, dc) for j in range(ROWS) for dz in range(2) for part in range(2) for dc in range(2)]

    def in_copy(n):
        j, dz, part, dc = order[n]
        return pltpu.make_async_copy(kv_refs[n], kvs.at[slot_of(j, dz, dc), part], in_sem.at[n])

    for n in range(len(order)):
        in_copy(n).start()

    base = (row - 2) * (4 * BLK)
    first = base + (8 + place) * BLK
    q_pos = lax.broadcasted_iota(jnp.int32, (1, BLK), 1) + (8 + place) * BLK
    starts = jnp.zeros((1, BLK), jnp.int32) - base
    first_start = -base
    last_start = -base
    end = jnp.int32(0)
    for c in range(16):
        end = end + len_ref[c]
        rel = end - base
        starts = jnp.where(q_pos >= rel, rel, starts)
        first_start = jnp.where(end <= first, rel, first_start)
        last_start = jnp.where(end <= first + BLK - 1, rel, last_start)
    lo = first_start // BLK
    hi = 8 + place

    for h in range(HEADS):
        cols = slice(h * BLK, (h + 1) * BLK)
        qt[:, cols] = q_ref[h].T
        dot_t[:, cols] = do_ref[h].T
    row_max[...] = jnp.zeros((1, NQ), F32)
    total[...] = jnp.zeros((1, NQ), F32)
    acc[...] = jnp.zeros((HD, NQ), F32)
    dq_acc[...] = jnp.zeros((HD, NQ), F32)
    q_norm = jnp.max(dot(jnp.ones((8, HD), BF16), jnp.square(qt[...].astype(F32)).astype(BF16)))
    for n in range(len(order)):
        in_copy(n).wait()

    def norm_step(t, k_norm):
        norms = dot(jnp.square(kvs[t, 0].astype(F32)).astype(BF16), jnp.ones((HD, HD), BF16))
        return jnp.maximum(k_norm, jnp.max(norms.reshape(BLK // 8, 8, HD), axis=0))

    k_norm = jnp.max(lax.fori_loop(lo, hi + 1, norm_step, jnp.zeros((8, HD), F32)))
    safe = q_norm * k_norm <= 0.98 * (BOUND / LOG2) ** 2

    def tile_mask(t):
        k_pos = lax.broadcasted_iota(jnp.int32, (BLK, BLK), 0) + t * BLK
        return (k_pos >= starts) & (k_pos <= q_pos)

    def max_step(t, carry):
        allowed = tile_mask(t)
        for h in range(HEADS):
            cols = slice(h * BLK, (h + 1) * BLK)
            s = jnp.where(allowed, dot(kvs[t, 0], qt[:, cols]), NEGATIVE)
            row_max[:, cols] = jnp.maximum(row_max[:, cols], jnp.max(s, axis=0, keepdims=True))
        return carry

    @pl.when(jnp.logical_not(safe))
    def _():
        row_max[...] = jnp.full((1, NQ), NEGATIVE, F32)
        lax.fori_loop(lo, hi + 1, max_step, 0)
        row_max[...] = row_max[...] * LOG2

    def forward(t, masked):
        k = kvs[t, 0]
        v_t = kvs[t, 1].T
        if masked:
            allowed = tile_mask(t)
        def score(h):
            s = dot(k, qt[:, h * HALF:(h + 1) * HALF])
            return jnp.where(allowed[:, (h % 2) * HALF:(h % 2 + 1) * HALF], s, NEGATIVE) if masked else s

        def soft(h, s):
            cols = slice(h * HALF, (h + 1) * HALF)
            p = jnp.exp2(s * LOG2 - row_max[:, cols])
            total[:, cols] += jnp.sum(p, axis=0, keepdims=True)
            p = p.astype(BF16)
            probs[t - lo, :, cols] = p
            return p

        def pv(h, p):
            cols = slice(h * HALF, (h + 1) * HALF)
            acc[:, cols] += dot(v_t, p)

        weights = soft(0, score(0))
        s = score(1)
        for h in range(1, 2 * HEADS):
            held, weights = weights, soft(h, s)
            if h + 1 < 2 * HEADS:
                s = score(h + 1)
            pv(h - 1, held)
        pv(2 * HEADS - 1, weights)

    def forward_step(t, carry):
        masked = (t * BLK < last_start) | (t == hi)

        @pl.when(masked)
        def _():
            forward(t, True)

        @pl.when(jnp.logical_not(masked))
        def _():
            forward(t, False)

        return carry

    lax.fori_loop(lo, hi + 1, forward_step, 0)

    for h in range(HEADS):
        cols = slice(h * BLK, (h + 1) * BLK)
        inverse = 1.0 / total[:, cols]
        o = (acc[:, cols] * inverse).astype(BF16)
        o_ref[h] = o.T
        scaled = (dot_t[:, cols].astype(F32) * inverse).astype(BF16)
        dot_t[:, cols] = scaled
        do_s[h * BLK:(h + 1) * BLK] = scaled.T
        delta[:, cols] = jnp.sum(o.astype(F32) * scaled.astype(F32), axis=0, keepdims=True)

    def out_copy(n, t):
        j, dz, part, dc = order[n]
        return pltpu.make_async_copy(dkvs.at[t, part], out_refs[part * 2 + dc].at[j, dz], out_sem.at[n])

    def send_out(t):
        for n, (j, dz, part, dc) in enumerate(order):
            if part == 0:
                @pl.when(slot_of(j, dz, dc) == t)
                def _():
                    out_copy(n, t).start()
                    out_copy(n + 2, t).start()

    dkvs[SLOTS] = jnp.zeros((2, BLK, HD), BF16)
    for n, (j, dz, part, dc) in enumerate(order):
        slot = slot_of(j, dz, dc)

        @pl.when((slot < lo) | (slot > hi))
        def _():
            out_copy(n, SLOTS).start()

    def backward_step(t, carry):
        k_t = kvs[t, 0].T
        v = kvs[t, 1]
        def dp_of(h):
            return dot(v, dot_t[:, h * BLK:(h + 1) * BLK])

        def ds_of(h, dp):
            cols = slice(h * BLK, (h + 1) * BLK)
            ds = (probs[t - lo, :, cols].astype(F32) * (dp - delta[:, cols])).astype(BF16)
            stage_s[:, cols] = ds
            return ds

        def dq_of(h, ds):
            dq_acc[:, h * BLK:(h + 1) * BLK] += dot(k_t, ds)

        d0 = dp_of(0)
        d1 = dp_of(1)
        s0 = ds_of(0, d0)
        dkvs[t, 1] = dot(probs[t - lo], do_s[...]).astype(BF16)
        d2 = dp_of(2)
        dq_of(0, s0)
        s1 = ds_of(1, d1)
        d3 = dp_of(3)
        dq_of(1, s1)
        s2 = ds_of(2, d2)
        dq_of(2, s2)
        s3 = ds_of(3, d3)
        dq_of(3, s3)
        dkvs[t, 0] = (dot(stage_s[...], q_ref[...].reshape(NQ, HD)) * SCALE).astype(BF16)
        send_out(t)
        return carry

    lax.fori_loop(lo, hi + 1, backward_step, 0)

    copies = [out_copy(n, 0) for n in range(len(order))]
    for h in range(HEADS):
        cols = slice(h * BLK, (h + 1) * BLK)
        dq_ref[h] = (dq_acc[:, cols] * SCALE).astype(BF16).T
    for copy in copies:
        copy.wait()


def attention(seq_lengths, queries, d_out, blocks):
    vmem = pl.BlockSpec(memory_space=pltpu.VMEM)
    anywhere = pl.BlockSpec(memory_space=pl.ANY)
    grads = jax.ShapeDtypeStruct((ROWS, 2, BLK, HD), BF16)
    rows = jax.ShapeDtypeStruct((HEADS, BLK, HD), BF16)
    return pl.pallas_call(
        attention_kernel,
        out_shape=(rows, rows) + (grads,) * 4,
        in_specs=[pl.BlockSpec(memory_space=pltpu.SMEM), vmem, vmem] + [anywhere] * 24,
        out_specs=[vmem, vmem] + [anywhere] * 4,
        scratch_shapes=[
            pltpu.VMEM((SLOTS, 2, BLK, HD), BF16),
            pltpu.VMEM((SLOTS + 1, 2, BLK, HD), BF16),
            pltpu.VMEM((HD, NQ), BF16),
            pltpu.VMEM((HD, NQ), BF16),
            pltpu.VMEM((NQ, HD), BF16),
            pltpu.VMEM((SPAN, BLK, NQ), BF16),
            pltpu.VMEM((1, NQ), F32),
            pltpu.VMEM((1, NQ), F32),
            pltpu.VMEM((HD, NQ), F32),
            pltpu.VMEM((HD, NQ), F32),
            pltpu.VMEM((BLK, NQ), BF16),
            pltpu.VMEM((1, NQ), F32),
            pltpu.SemaphoreType.DMA((2 * SLOTS,)),
            pltpu.SemaphoreType.DMA((2 * SLOTS,)),
        ],
        compiler_params=pltpu.CompilerParams(vmem_limit_bytes=56 << 20),
        cost_estimate=pl.CostEstimate(flops=8 << 30, bytes_accessed=16 << 20, transcendentals=9 << 20),
        name="attention",
    )(seq_lengths, queries, d_out, *blocks)


def swap_core(value):
    return lax.ppermute(value, "core", [(0, 1), (1, 0)])


def swap_z(value, sources=(0, 1)):
    pairs = [(2 * zh + zl, 2 * (1 - zh) + (1 - zl)) for zh in sources for zl in range(2)]
    return lax.ppermute(value, ("zh", "zl"), pairs)


def swap_head(value):
    return lax.ppermute(value, "zl", [(0, 1), (1, 0)])


def shift_row(value, by):
    return lax.ppermute(value, ("x", "y"), [(r, (r + by) % 16) for r in range(16)])


def added(*values):
    total = values[0].astype(F32)
    for value in values[1:]:
        total = total + value.astype(F32)
    return total.astype(BF16)


def gathered(own):
    row1 = shift_row(own, 1)
    side0 = swap_z(own, (0,))
    row1, side0 = lax.optimization_barrier((row1, side0))
    row2 = shift_row(row1, 1)
    side1 = swap_z(row1)
    row2, side1 = lax.optimization_barrier((row2, side1))
    side2 = swap_z(row2, (1,))
    return [(block, swap_core(block)) for block in (own, side0, row1, side1, row2, side2)]


def returned(keep, send):
    first = lax.axis_index("zh") == 0
    given = swap_core(send)
    outer = swap_z(added(jnp.where(first, keep[2, 1], keep[0, 1]), jnp.where(first, given[2, 1], given[0, 1])))
    middle = swap_z(added(keep[1, 1], given[1, 1]))
    zero = jnp.zeros((), BF16)
    back = shift_row(added(keep[2, 0], given[2, 0], jnp.where(first, zero, outer)), -1)
    back = shift_row(added(keep[1, 0], given[1, 0], middle, back), -1)
    half = added(keep[0, 0], given[0, 0], jnp.where(first, outer, zero), back)
    return added(half, swap_head(half))


def on_device(queries, key_rows, value_rows, d_out, seq_lengths):
    blocks = []
    for keys, values in zip(gathered(key_rows), gathered(value_rows)):
        blocks += [*keys, *values]
    attended, grad_queries, *parts = attention(seq_lengths, queries, d_out, blocks)
    return attended, grad_queries, returned(*parts[:2]), returned(*parts[2:])


def solution(mesh):
    fine = Mesh(mesh.devices.reshape(4, 4, 2, 2, 2), ("x", "y", "zh", "core", "zl"))
    tokens = P("zl", SEQ, None)
    rows = P(SEQ, None)
    return jax.shard_map(
        on_device,
        mesh=fine,
        in_specs=(tokens, rows, rows, tokens, P()),
        out_specs=(tokens, tokens, rows, rows),
        check_vma=False,
    )
```

```python
import math

import jax
import jax.numpy as jnp
from jax import lax
from jax.experimental import pallas as pl
from jax.experimental.pallas import tpu as pltpu
from jax.sharding import Mesh, PartitionSpec as P

NEGATIVE = -1e30
BLK = 512
HEADS = 4
HD = 128
NQ = HEADS * BLK
HALF = BLK // 2
ROWS = 3
SLOTS = 4 * ROWS
SCALE = HD ** -0.5
LOG2 = SCALE * math.log2(math.e)
BOUND = 64.0
F32 = jnp.float32
BF16 = jnp.bfloat16
SEQ = ("x", "y", "zh", "core")
VMEM = pl.BlockSpec(memory_space=pltpu.VMEM)
SMEM = pl.BlockSpec(memory_space=pltpu.SMEM)
ANY = pl.BlockSpec(memory_space=pl.ANY)
DMA = pltpu.SemaphoreType.DMA
NEAR = [(dz, dc) for dz in range(2) for dc in range(2)]


def shape(dims, dtype):
    return jax.ShapeDtypeStruct(dims, dtype)


def params(flops):
    return dict(
        compiler_params=pltpu.CompilerParams(vmem_limit_bytes=56 << 20),
        cost_estimate=pl.CostEstimate(flops=flops, bytes_accessed=16 << 20, transcendentals=4 << 20),
    )


def dot(a, b):
    return lax.dot_general(a, b, (((1,), (0,)), ((), ())), preferred_element_type=F32)


class Place:
    def __init__(self, len_ref):
        row = lax.axis_index("x") * 4 + lax.axis_index("y")
        self.zh = lax.axis_index("zh")
        self.core = lax.axis_index("core")
        place = self.zh * 2 + self.core
        base = (row - 2) * (4 * BLK)
        first = base + (8 + place) * BLK
        self.q_pos = lax.broadcasted_iota(jnp.int32, (1, BLK), 1) + (8 + place) * BLK
        starts = jnp.zeros((1, BLK), jnp.int32) - base
        first_start = -base
        last_start = -base
        end = jnp.int32(0)
        for c in range(16):
            end = end + len_ref[c]
            rel = end - base
            starts = jnp.where(self.q_pos >= rel, rel, starts)
            first_start = jnp.where(end <= first, rel, first_start)
            last_start = jnp.where(end <= first + BLK - 1, rel, last_start)
        self.starts = starts
        self.last_start = last_start
        self.lo = first_start // BLK
        self.hi = 8 + place

    def slot(self, j, dz, dc):
        return (2 - j) * 4 + (1 - self.zh if dz else self.zh) * 2 + (1 - self.core if dc else self.core)

    def span(self, rows):
        return jnp.maximum(self.lo, (2 - max(rows)) * 4), jnp.minimum(self.hi + 1, (3 - min(rows)) * 4)

    def mask(self, t):
        k_pos = lax.broadcasted_iota(jnp.int32, (BLK, BLK), 0) + t * BLK
        return (k_pos >= self.starts) & (k_pos <= self.q_pos)


class Fetch:
    def __init__(self, at, rows, refs, kvs, sem, base):
        order = [(j, dz, dc) for j in rows for dz, dc in NEAR]
        self.copies = [
            pltpu.make_async_copy(refs[n], kvs.at[at.slot(*where) - base], sem.at[n]) for n, where in enumerate(order)
        ]
        for copy in self.copies:
            copy.start()

    def wait(self):
        for copy in self.copies:
            copy.wait()


def transposed(q_ref, qt):
    for h in range(HEADS):
        qt[:, h * BLK:(h + 1) * BLK] = q_ref[h].T


def forward_rows(at, begin, end, base, kvs, qt, probs, row_max, total, acc, norms, finish=None, settle=None):
    def forward(t, masked):
        k = kvs[t - base, 0]
        v_t = kvs[t - base, 1].T
        squares = dot(jnp.square(k.astype(F32)).astype(BF16), jnp.ones((HD, HD), BF16))
        norms[...] = jnp.maximum(norms[...], jnp.max(squares.reshape(BLK // 8, 8, HD), axis=0))
        if masked:
            allowed = at.mask(t)

        def score(h):
            s = dot(k, qt[:, h * HALF:(h + 1) * HALF])
            return jnp.where(allowed[:, (h % 2) * HALF:(h % 2 + 1) * HALF], s, NEGATIVE) if masked else s

        def soft(h, s):
            cols = slice(h * HALF, (h + 1) * HALF)
            p = jnp.exp2(s * LOG2 - row_max[:, cols])
            total[:, cols] += jnp.sum(p, axis=0, keepdims=True)
            p = p.astype(BF16)
            probs[t - base, :, cols] = p
            return p

        def product(h, p):
            acc[:, h * HALF:(h + 1) * HALF] += dot(v_t, p)

        weights = soft(0, score(0))
        s = score(1)
        for h in range(1, 2 * HEADS):
            held, weights = weights, soft(h, s)
            if h + 1 < 2 * HEADS:
                s = score(h + 1)
            product(h - 1, held)
        product(2 * HEADS - 1, weights)

    def step(t, carry):
        masked = (t * BLK < at.last_start) | (t == at.hi)

        @pl.when(masked)
        def _():
            forward(t, True)

        @pl.when(jnp.logical_not(masked))
        def _():
            forward(t, False)

        if finish is not None:
            finish(t)
        return carry

    def run():
        total[...] = jnp.zeros((1, NQ), F32)
        acc[...] = jnp.zeros((HD, NQ), F32)
        lax.fori_loop(begin, end, step, 0)

    def max_step(t, carry):
        allowed = at.mask(t)
        for h in range(HEADS):
            cols = slice(h * BLK, (h + 1) * BLK)
            s = jnp.where(allowed, dot(kvs[t - base, 0], qt[:, cols]), NEGATIVE)
            row_max[:, cols] = jnp.maximum(row_max[:, cols], jnp.max(s, axis=0, keepdims=True))
        return carry

    q_norm = jnp.max(dot(jnp.ones((8, HD), BF16), jnp.square(qt[...].astype(F32)).astype(BF16)))
    norms[...] = jnp.zeros((8, HD), F32)
    row_max[...] = jnp.zeros((1, NQ), F32)
    run()

    @pl.when(q_norm * jnp.max(norms[...]) > 0.98 * (BOUND / LOG2) ** 2)
    def _():
        if settle is not None:
            settle()
        row_max[...] = jnp.full((1, NQ), NEGATIVE, F32)
        lax.fori_loop(begin, end, max_step, 0)
        row_max[...] = row_max[...] * LOG2
        run()


def backward_rows(at, begin, end, base, rows, kvs, q_ref, dot_t, do_s, delta, probs, stage, dq_acc, dkvs, out_refs, out_sem, ready=None):
    order = [(j, dz, dc) for j in rows for dz, dc in NEAR]
    spare = 4 * len(rows)

    def out_copy(n, t):
        j, dz, dc = order[n]
        return pltpu.make_async_copy(dkvs.at[t - base], out_refs[dc].at[rows.index(j), dz], out_sem.at[n])

    dkvs[spare] = jnp.zeros((2, BLK, HD), BF16)
    for n, where in enumerate(order):
        slot = at.slot(*where)

        @pl.when((slot < begin) | (slot >= end))
        def _():
            out_copy(n, base + spare).start()

    def step(t, carry):
        if ready is not None:
            ready(t)
        k_t = kvs[t - base, 0].T
        v = kvs[t - base, 1]

        def dp_of(h):
            return dot(v, dot_t[:, h * BLK:(h + 1) * BLK])

        def ds_of(h, dp):
            cols = slice(h * BLK, (h + 1) * BLK)
            ds = (probs[t - base, :, cols].astype(F32) * (dp - delta[:, cols])).astype(BF16)
            stage[:, cols] = ds
            return ds

        def dq_of(h, ds):
            dq_acc[:, h * BLK:(h + 1) * BLK] += dot(k_t, ds)

        d0 = dp_of(0)
        d1 = dp_of(1)
        s0 = ds_of(0, d0)
        dkvs[t - base, 1] = dot(probs[t - base], do_s[...]).astype(BF16)
        d2 = dp_of(2)
        dq_of(0, s0)
        s1 = ds_of(1, d1)
        d3 = dp_of(3)
        dq_of(1, s1)
        s2 = ds_of(2, d2)
        dq_of(2, s2)
        s3 = ds_of(3, d3)
        dq_of(3, s3)
        dkvs[t - base, 0] = (dot(stage[...], q_ref[...].reshape(NQ, HD)) * SCALE).astype(BF16)
        for n, where in enumerate(order):
            @pl.when(at.slot(*where) == t)
            def _():
                out_copy(n, t).start()

        return carry

    lax.fori_loop(begin, end, step, 0)

    def wait():
        for n in range(len(order)):
            out_copy(n, base).wait()

    return wait


def forward_kernel(*refs):
    len_ref, q_ref = refs[:2]
    kv_refs = refs[2:10]
    p_out, row_max, total, acc = refs[10:14]
    kvs, qt, probs, norms, in_sem, out_sem = refs[14:]
    at = Place(len_ref)
    fetch = Fetch(at, (0, 1), kv_refs, kvs, in_sem, 4)
    transposed(q_ref, qt)
    begin, end = at.span((0, 1))

    def out_copy(t):
        return pltpu.make_async_copy(probs.at[t - 4], p_out.at[t - 4], out_sem.at[t - 4])

    def settle():
        def wait(t, carry):
            out_copy(t).wait()
            return carry

        lax.fori_loop(begin, end, wait, 0)

    fetch.wait()
    forward_rows(
        at, begin, end, 4, kvs, qt, probs, row_max, total, acc, norms, lambda t: out_copy(t).start(), settle
    )
    settle()


def forward_call(seq_lengths, queries, blocks):
    return pl.pallas_call(
        forward_kernel,
        out_shape=(shape((8, BLK, NQ), BF16), shape((1, NQ), F32), shape((1, NQ), F32), shape((HD, NQ), F32)),
        in_specs=[SMEM, VMEM] + [ANY] * 8,
        out_specs=[ANY, VMEM, VMEM, VMEM],
        scratch_shapes=[
            pltpu.VMEM((8, 2, BLK, HD), BF16),
            pltpu.VMEM((HD, NQ), BF16),
            pltpu.VMEM((8, BLK, NQ), BF16),
            pltpu.VMEM((8, HD), F32),
            DMA((8,)),
            DMA((8,)),
        ],
        name="forward_near",
        **params(3 << 30),
    )(seq_lengths, queries, *blocks)


def middle_kernel(*refs):
    len_ref, q_ref, do_ref, max_near, total_near, acc_near = refs[:6]
    kv_refs = refs[6:10]
    o_ref, dot_t, do_s, delta, dq_acc = refs[10:15]
    out_refs = refs[15:17]
    kvs, dkvs, qt, probs, row_max, total, acc, norms, far_dot_t, far_do_s, far_delta, stage, in_sem, out_sem = refs[17:]
    at = Place(len_ref)
    fetch = Fetch(at, (2,), kv_refs, kvs, in_sem, 0)
    transposed(q_ref, qt)
    begin, end = at.span((2,))
    fetch.wait()
    forward_rows(at, begin, end, 0, kvs, qt, probs, row_max, total, acc, norms)
    for h in range(HEADS):
        cols = slice(h * BLK, (h + 1) * BLK)
        top = jnp.maximum(row_max[:, cols], max_near[:, cols])
        far = jnp.exp2(row_max[:, cols] - top)
        near = jnp.exp2(max_near[:, cols] - top)
        inverse = 1.0 / (far * total[:, cols] + near * total_near[:, cols])
        far = far * inverse
        near = near * inverse
        o = (acc[:, cols] * far + acc_near[:, cols] * near).astype(BF16)
        o_ref[h] = o.T
        o = o.astype(F32)
        grad = do_ref[h].T.astype(F32)
        for factor, t_ref, n_ref, d_ref in ((near, dot_t, do_s, delta), (far, far_dot_t, far_do_s, far_delta)):
            scaled = (grad * factor).astype(BF16)
            t_ref[:, cols] = scaled
            n_ref[h * BLK:(h + 1) * BLK] = scaled.T
            d_ref[:, cols] = jnp.sum(o * scaled.astype(F32), axis=0, keepdims=True)
    dq_acc[...] = jnp.zeros((HD, NQ), F32)
    wait = backward_rows(
        at, begin, end, 0, (2,), kvs, q_ref, far_dot_t, far_do_s, far_delta, probs, stage, dq_acc, dkvs, out_refs, out_sem
    )
    wait()


def middle_call(seq_lengths, queries, d_out, row_max, total, acc, blocks):
    grads = shape((1, 2, 2, BLK, HD), BF16)
    return pl.pallas_call(
        middle_kernel,
        out_shape=(
            shape((HEADS, BLK, HD), BF16),
            shape((HD, NQ), BF16),
            shape((NQ, HD), BF16),
            shape((1, NQ), F32),
            shape((HD, NQ), F32),
            grads,
            grads,
        ),
        in_specs=[SMEM] + [VMEM] * 5 + [ANY] * 4,
        out_specs=[VMEM] * 5 + [ANY] * 2,
        scratch_shapes=[
            pltpu.VMEM((4, 2, BLK, HD), BF16),
            pltpu.VMEM((5, 2, BLK, HD), BF16),
            pltpu.VMEM((HD, NQ), BF16),
            pltpu.VMEM((4, BLK, NQ), BF16),
            pltpu.VMEM((1, NQ), F32),
            pltpu.VMEM((1, NQ), F32),
            pltpu.VMEM((HD, NQ), F32),
            pltpu.VMEM((8, HD), F32),
            pltpu.VMEM((HD, NQ), BF16),
            pltpu.VMEM((NQ, HD), BF16),
            pltpu.VMEM((1, NQ), F32),
            pltpu.VMEM((BLK, NQ), BF16),
            DMA((4,)),
            DMA((4,)),
        ],
        name="middle_far",
        **params(5 << 30),
    )(seq_lengths, queries, d_out, row_max, total, acc, *blocks)


def backward_call(seq_lengths, queries, dot_t, do_s, delta, dq_in, probs, blocks, rows, last):
    count = 4 * len(rows)
    base = (2 - max(rows)) * 4

    def kernel(*refs):
        len_ref, q_ref, dot_ref, do_ref, delta_ref, dq_ref, p_in = refs[:7]
        kv_refs = refs[7:7 + count]
        dq_out = refs[7 + count]
        out_refs = refs[8 + count:10 + count]
        kvs, dkvs, tiles, stage, dq_acc, in_sem, p_sem, out_sem = refs[10 + count:]
        at = Place(len_ref)
        fetch = Fetch(at, rows, kv_refs, kvs, in_sem, base)
        begin, end = at.span(rows)

        def p_copy(t):
            return pltpu.make_async_copy(p_in.at[t - 4], tiles.at[t - base], p_sem.at[t - base])

        def start(t, carry):
            p_copy(t).start()
            return carry

        lax.fori_loop(begin, end, start, 0)
        dq_acc[...] = dq_ref[...]
        fetch.wait()
        wait = backward_rows(
            at, begin, end, base, rows, kvs, q_ref, dot_ref, do_ref, delta_ref, tiles, stage, dq_acc, dkvs, out_refs,
            out_sem, lambda t: p_copy(t).wait()
        )
        if last:
            for h in range(HEADS):
                dq_out[h] = (dq_acc[:, h * BLK:(h + 1) * BLK] * SCALE).astype(BF16).T
        else:
            dq_out[...] = dq_acc[...]
        wait()

    grads = shape((len(rows), 2, 2, BLK, HD), BF16)
    return pl.pallas_call(
        kernel,
        out_shape=(shape((HEADS, BLK, HD), BF16) if last else shape((HD, NQ), F32), grads, grads),
        in_specs=[SMEM] + [VMEM] * 5 + [ANY] * (1 + count),
        out_specs=[VMEM, ANY, ANY],
        scratch_shapes=[
            pltpu.VMEM((count, 2, BLK, HD), BF16),
            pltpu.VMEM((count + 1, 2, BLK, HD), BF16),
            pltpu.VMEM((count, BLK, NQ), BF16),
            pltpu.VMEM((BLK, NQ), BF16),
            pltpu.VMEM((HD, NQ), F32),
            DMA((count,)),
            DMA((count,)),
            DMA((count,)),
        ],
        name="backward_rows",
        **params(3 << 30),
    )(seq_lengths, queries, dot_t, do_s, delta, dq_in, probs, *blocks)


def swap_core(value):
    return lax.ppermute(value, "core", [(0, 1), (1, 0)])


def swap_z(value, sources=(0, 1)):
    pairs = [(2 * zh + zl, 2 * (1 - zh) + (1 - zl)) for zh in sources for zl in range(2)]
    return lax.ppermute(value, ("zh", "zl"), pairs)


def swap_head(value):
    return lax.ppermute(value, "zl", [(0, 1), (1, 0)])


def shift_row(value, by):
    return lax.ppermute(value, ("x", "y"), [(r, (r + by) % 16) for r in range(16)])


def added(*values):
    total = values[0].astype(F32)
    for value in values[1:]:
        total = total + value.astype(F32)
    return total.astype(BF16)


def on_device(queries, key_rows, value_rows, d_out, seq_lengths):
    own = jnp.stack([key_rows, value_rows])
    row1 = shift_row(own, 1)
    side0 = swap_z(own, (0,))
    row1, side0 = lax.optimization_barrier((row1, side0))
    row2 = shift_row(row1, 1)
    side1 = swap_z(row1)
    side2 = swap_z(row2, (1,))
    near = []
    for block in (own, side0, row1, side1):
        near += [block, swap_core(block)]
    far = []
    for block in (row2, side2):
        far += [block, swap_core(block)]
    probs, row_max, total, acc = forward_call(seq_lengths, queries, near)
    attended, dot_t, do_s, delta, dq, keep2, send2 = middle_call(
        seq_lengths, queries, d_out, row_max, total, acc, far
    )
    given = swap_core(send2)
    here2, there2 = (added(keep2[0, dz], given[0, dz]) for dz in range(2))
    dq, here2, there2 = lax.optimization_barrier((dq, here2, there2))
    side2 = swap_z(there2, (0,))
    dq, keep1, send1 = backward_call(seq_lengths, queries, dot_t, do_s, delta, dq, probs, near[4:], (1,), False)
    given = swap_core(send1)
    here1, there1 = ([added(keep1[0, dz, part], given[0, dz, part]) for part in range(2)] for dz in range(2))
    sum2 = added(here2, side2)
    dq, here1, there1, sum2 = lax.optimization_barrier((dq, here1, there1, sum2))
    back2 = shift_row(sum2, -1)
    side1 = [swap_z(there) for there in there1]
    dq, keep0, send0 = backward_call(seq_lengths, queries, dot_t, do_s, delta, dq, probs, near[:4], (0,), True)
    given = swap_core(send0)
    outs = []
    for part in range(2):
        here0, there0 = (added(keep0[0, dz, part], given[0, dz, part]) for dz in range(2))
        back1 = shift_row(added(here1[part], side1[part], back2[part]), -1)
        half = added(here0, swap_z(there0, (1,)), back1)
        outs.append(added(half, swap_head(half)))
    return attended, dq, outs[0], outs[1]


def solution(mesh):
    fine = Mesh(mesh.devices.reshape(4, 4, 2, 2, 2), ("x", "y", "zh", "core", "zl"))
    tokens = P("zl", SEQ, None)
    rows = P(SEQ, None)
    return jax.shard_map(
        on_device,
        mesh=fine,
        in_specs=(tokens, rows, rows, tokens, P()),
        out_specs=(tokens, tokens, rows, rows),
        check_vma=False,
    )
```

```python
import math

import jax
import jax.numpy as jnp
from jax import lax
from jax.experimental import pallas as pl
from jax.experimental.pallas import tpu as pltpu
from jax.sharding import Mesh, PartitionSpec as P

NEGATIVE = -1e30
BLK = 512
HEADS = 4
HD = 128
NQ = HEADS * BLK
HALF = BLK // 2
ROWS = 3
SLOTS = 4 * ROWS
SPAN = 9
SCALE = HD ** -0.5
LOG2 = SCALE * math.log2(math.e)
BOUND = 64.0
F32 = jnp.float32
BF16 = jnp.bfloat16
SEQ = ("x", "y", "zh", "core")
VMEM = pl.BlockSpec(memory_space=pltpu.VMEM)
SMEM = pl.BlockSpec(memory_space=pltpu.SMEM)
ANY = pl.BlockSpec(memory_space=pl.ANY)
DMA = pltpu.SemaphoreType.DMA
NEAR = [(dz, dc) for dz in range(2) for dc in range(2)]


def shape(dims, dtype):
    return jax.ShapeDtypeStruct(dims, dtype)


def dot(a, b):
    return lax.dot_general(a, b, (((1,), (0,)), ((), ())), preferred_element_type=F32)


class Place:
    def __init__(self, len_ref):
        row = lax.axis_index("x") * 4 + lax.axis_index("y")
        self.zh = lax.axis_index("zh")
        self.core = lax.axis_index("core")
        place = self.zh * 2 + self.core
        base = (row - 2) * (4 * BLK)
        first = base + (8 + place) * BLK
        self.q_pos = lax.broadcasted_iota(jnp.int32, (1, BLK), 1) + (8 + place) * BLK
        starts = jnp.zeros((1, BLK), jnp.int32) - base
        first_start = -base
        last_start = -base
        end = jnp.int32(0)
        for c in range(16):
            end = end + len_ref[c]
            rel = end - base
            starts = jnp.where(self.q_pos >= rel, rel, starts)
            first_start = jnp.where(end <= first, rel, first_start)
            last_start = jnp.where(end <= first + BLK - 1, rel, last_start)
        self.starts = starts
        self.last_start = last_start
        self.lo = first_start // BLK
        self.hi = 8 + place

    def slot(self, j, dz, dc):
        return (2 - j) * 4 + (1 - self.zh if dz else self.zh) * 2 + (1 - self.core if dc else self.core)

    def mask(self, t):
        k_pos = lax.broadcasted_iota(jnp.int32, (BLK, BLK), 0) + t * BLK
        return (k_pos >= self.starts) & (k_pos <= self.q_pos)


def attention_kernel(*refs):
    len_ref, q_ref, do_ref = refs[:3]
    kv_refs = refs[3:15]
    o_ref, dq_ref = refs[15:17]
    out_refs = refs[17:21]
    kvs, dkvs, qt, dot_t, do_s, probs, row_max, total, acc, dq_acc, stage, delta, norms, in_sem, out_sem = refs[21:]
    at = Place(len_ref)
    order = [(j, dz, dc) for j in range(ROWS) for dz, dc in NEAR]
    for n, where in enumerate(order):
        slot = at.slot(*where)
        pltpu.make_async_copy(kv_refs[n], kvs.at[slot], in_sem.at[slot]).start()

    def arrived(t):
        pltpu.make_async_copy(kv_refs[0], kvs.at[t], in_sem.at[t]).wait()

    def out_copy(n, part, t):
        j, dz, dc = order[n]
        return pltpu.make_async_copy(dkvs.at[t, part], out_refs[part * 2 + dc].at[j, dz], out_sem.at[n, part])

    begin, end = at.lo, at.hi + 1
    dkvs[SLOTS] = jnp.zeros((2, BLK, HD), BF16)
    for n, where in enumerate(order):
        slot = at.slot(*where)

        @pl.when((slot < begin) | (slot >= end))
        def _():
            for part in range(2):
                out_copy(n, part, SLOTS).start()

    for h in range(HEADS):
        cols = slice(h * BLK, (h + 1) * BLK)
        qt[:, cols] = q_ref[h].T
        dot_t[:, cols] = do_ref[h].T
    dq_acc[...] = jnp.zeros((HD, NQ), F32)
    norms[...] = jnp.zeros((8, HD), F32)

    def forward(t, masked, shift):
        k = kvs[t, 0]
        v_t = kvs[t, 1].T
        if not shift:
            squares = dot(jnp.square(k.astype(F32)).astype(BF16), jnp.ones((HD, HD), BF16))
            norms[...] = jnp.maximum(norms[...], jnp.max(squares.reshape(BLK // 8, 8, HD), axis=0))
        if masked:
            allowed = at.mask(t)

        def score(h):
            s = dot(k, qt[:, h * HALF:(h + 1) * HALF])
            return jnp.where(allowed[:, (h % 2) * HALF:(h % 2 + 1) * HALF], s, NEGATIVE) if masked else s

        def soft(h, s):
            cols = slice(h * HALF, (h + 1) * HALF)
            p = jnp.exp2(s * LOG2 - row_max[:, cols] if shift else s * LOG2)
            total[:, cols] += jnp.sum(p, axis=0, keepdims=True)
            p = p.astype(BF16)
            probs[t - begin, :, cols] = p
            return p

        def product(h, p):
            acc[:, h * HALF:(h + 1) * HALF] += dot(v_t, p)

        weights = soft(0, score(0))
        s = score(1)
        for h in range(1, 2 * HEADS):
            held, weights = weights, soft(h, s)
            if h + 1 < 2 * HEADS:
                s = score(h + 1)
            product(h - 1, held)
        product(2 * HEADS - 1, weights)

    def clear():
        total[...] = jnp.zeros((1, NQ), F32)
        acc[...] = jnp.zeros((HD, NQ), F32)

    def fast_step(t, carry):
        arrived(t)
        masked = (t * BLK < at.last_start) | (t == at.hi)

        @pl.when(masked)
        def _():
            forward(t, True, False)

        @pl.when(jnp.logical_not(masked))
        def _():
            forward(t, False, False)

        return carry

    def max_step(t, carry):
        allowed = at.mask(t)
        for h in range(HEADS):
            cols = slice(h * BLK, (h + 1) * BLK)
            s = jnp.where(allowed, dot(kvs[t, 0], qt[:, cols]), NEGATIVE)
            row_max[:, cols] = jnp.maximum(row_max[:, cols], jnp.max(s, axis=0, keepdims=True))
        return carry

    def slow_step(t, carry):
        forward(t, True, True)
        return carry

    clear()
    lax.fori_loop(begin, end, fast_step, 0)
    q_norm = jnp.max(dot(jnp.ones((8, HD), BF16), jnp.square(qt[...].astype(F32)).astype(BF16)))

    @pl.when(q_norm * jnp.max(norms[...]) > 0.98 * (BOUND / LOG2) ** 2)
    def _():
        clear()
        row_max[...] = jnp.full((1, NQ), NEGATIVE, F32)
        lax.fori_loop(begin, end, max_step, 0)
        row_max[...] = row_max[...] * LOG2
        lax.fori_loop(begin, end, slow_step, 0)

    for h in range(HEADS):
        cols = slice(h * BLK, (h + 1) * BLK)
        inverse = 1.0 / total[:, cols]
        o = (acc[:, cols] * inverse).astype(BF16)
        o_ref[h] = o.T
        scaled = (dot_t[:, cols].astype(F32) * inverse).astype(BF16)
        dot_t[:, cols] = scaled
        do_s[h * BLK:(h + 1) * BLK] = scaled.T
        delta[:, cols] = jnp.sum(o.astype(F32) * scaled.astype(F32), axis=0, keepdims=True)

    def backward_step(t, carry):
        k_t = kvs[t, 0].T
        v = kvs[t, 1]

        def dp_of(h):
            return dot(v, dot_t[:, h * BLK:(h + 1) * BLK])

        def ds_of(h, dp):
            cols = slice(h * BLK, (h + 1) * BLK)
            ds = (probs[t - begin, :, cols].astype(F32) * (dp - delta[:, cols])).astype(BF16)
            stage[:, cols] = ds
            return ds

        def dq_of(h, ds):
            dq_acc[:, h * BLK:(h + 1) * BLK] += dot(k_t, ds)

        d0 = dp_of(0)
        d1 = dp_of(1)
        s0 = ds_of(0, d0)
        dkvs[t, 1] = dot(probs[t - begin], do_s[...]).astype(BF16)
        d2 = dp_of(2)
        dq_of(0, s0)
        s1 = ds_of(1, d1)
        d3 = dp_of(3)
        dq_of(1, s1)
        s2 = ds_of(2, d2)
        dq_of(2, s2)
        s3 = ds_of(3, d3)
        dq_of(3, s3)
        dkvs[t, 0] = (dot(stage[...], q_ref[...].reshape(NQ, HD)) * SCALE).astype(BF16)

        for n, where in enumerate(order):
            @pl.when(at.slot(*where) == t)
            def _():
                for part in range(2):
                    out_copy(n, part, t).start()

        return carry

    lax.fori_loop(begin, end, backward_step, 0)
    for h in range(HEADS):
        dq_ref[h] = (dq_acc[:, h * BLK:(h + 1) * BLK] * SCALE).astype(BF16).T

    def rest(t, carry):
        arrived(t)
        return carry

    lax.fori_loop(0, begin, rest, 0)
    lax.fori_loop(end, SLOTS, rest, 0)
    for n in range(len(order)):
        for part in range(2):
            out_copy(n, part, 0).wait()


def attention(seq_lengths, queries, d_out, blocks):
    rows = shape((HEADS, BLK, HD), BF16)
    grads = shape((ROWS, 2, BLK, HD), BF16)
    return pl.pallas_call(
        attention_kernel,
        out_shape=(rows, rows) + (grads,) * 4,
        in_specs=[SMEM, VMEM, VMEM] + [ANY] * SLOTS,
        out_specs=[VMEM, VMEM] + [ANY] * 4,
        scratch_shapes=[
            pltpu.VMEM((SLOTS, 2, BLK, HD), BF16),
            pltpu.VMEM((SLOTS + 1, 2, BLK, HD), BF16),
            pltpu.VMEM((HD, NQ), BF16),
            pltpu.VMEM((HD, NQ), BF16),
            pltpu.VMEM((NQ, HD), BF16),
            pltpu.VMEM((SPAN, BLK, NQ), BF16),
            pltpu.VMEM((1, NQ), F32),
            pltpu.VMEM((1, NQ), F32),
            pltpu.VMEM((HD, NQ), F32),
            pltpu.VMEM((HD, NQ), F32),
            pltpu.VMEM((BLK, NQ), BF16),
            pltpu.VMEM((1, NQ), F32),
            pltpu.VMEM((8, HD), F32),
            DMA((SLOTS,)),
            DMA((SLOTS, 2)),
        ],
        compiler_params=pltpu.CompilerParams(vmem_limit_bytes=56 << 20),
        cost_estimate=pl.CostEstimate(flops=8 << 30, bytes_accessed=16 << 20, transcendentals=9 << 20),
        name="attention",
    )(seq_lengths, queries, d_out, *blocks)


def swap_core(value):
    return lax.ppermute(value, "core", [(0, 1), (1, 0)])


def swap_z(value, sources=(0, 1)):
    pairs = [(2 * zh + zl, 2 * (1 - zh) + (1 - zl)) for zh in sources for zl in range(2)]
    return lax.ppermute(value, ("zh", "zl"), pairs)


def swap_head(value):
    return lax.ppermute(value, "zl", [(0, 1), (1, 0)])


def shift_row(value, by):
    return lax.ppermute(value, ("x", "y"), [(r, (r + by) % 16) for r in range(16)])


def added(*values):
    total = values[0].astype(F32)
    for value in values[1:]:
        total = total + value.astype(F32)
    return total.astype(BF16)


def returned(keep, send):
    first = lax.axis_index("zh") == 0
    given = swap_core(send)
    outer = swap_z(added(jnp.where(first, keep[2, 1], keep[0, 1]), jnp.where(first, given[2, 1], given[0, 1])))
    middle = swap_z(added(keep[1, 1], given[1, 1]))
    zero = jnp.zeros((), BF16)
    back = shift_row(added(keep[2, 0], given[2, 0], jnp.where(first, zero, outer)), -1)
    back = shift_row(added(keep[1, 0], given[1, 0], middle, back), -1)
    half = added(keep[0, 0], given[0, 0], jnp.where(first, outer, zero), back)
    return added(half, swap_head(half))


def on_device(queries, key_rows, value_rows, d_out, seq_lengths):
    own = jnp.stack([key_rows, value_rows])
    row1 = shift_row(own, 1)
    side0 = swap_z(own, (0,))
    row1, side0 = lax.optimization_barrier((row1, side0))
    row2 = shift_row(row1, 1)
    side1 = swap_z(row1)
    row2, side1 = lax.optimization_barrier((row2, side1))
    side2 = swap_z(row2, (1,))
    blocks = []
    for block in (own, side0, row1, side1, row2, side2):
        blocks += [block, swap_core(block)]
    attended, grad_queries, *parts = attention(seq_lengths, queries, d_out, blocks)
    return attended, grad_queries, returned(*parts[:2]), returned(*parts[2:])


def solution(mesh):
    fine = Mesh(mesh.devices.reshape(4, 4, 2, 2, 2), ("x", "y", "zh", "core", "zl"))
    tokens = P("zl", SEQ, None)
    rows = P(SEQ, None)
    return jax.shard_map(
        on_device,
        mesh=fine,
        in_specs=(tokens, rows, rows, tokens, P()),
        out_specs=(tokens, tokens, rows, rows),
        check_vma=False,
    )
```

```python
import math

import jax
import jax.numpy as jnp
from jax import lax
from jax.experimental import pallas as pl
from jax.experimental.pallas import tpu as pltpu
from jax.sharding import Mesh, PartitionSpec as P

NEGATIVE = -1e30
BLK = 512
HEADS = 4
HD = 128
NQ = HEADS * BLK
HALF = BLK // 2
ROWS = 3
SLOTS = 4 * ROWS
SPAN = 9
SCALE = HD ** -0.5
LOG2 = SCALE * math.log2(math.e)
BOUND = 64.0
F32 = jnp.float32
BF16 = jnp.bfloat16
SEQ = ("x", "y", "zh", "core")
VMEM = pl.BlockSpec(memory_space=pltpu.VMEM)
SMEM = pl.BlockSpec(memory_space=pltpu.SMEM)
ANY = pl.BlockSpec(memory_space=pl.ANY)
DMA = pltpu.SemaphoreType.DMA
NEAR = [(dz, dc) for dz in range(2) for dc in range(2)]


def shape(dims, dtype):
    return jax.ShapeDtypeStruct(dims, dtype)


def dot(a, b):
    return lax.dot_general(a, b, (((1,), (0,)), ((), ())), preferred_element_type=F32)


class Place:
    def __init__(self, len_ref):
        row = lax.axis_index("x") * 4 + lax.axis_index("y")
        self.zh = lax.axis_index("zh")
        self.core = lax.axis_index("core")
        place = self.zh * 2 + self.core
        base = (row - 2) * (4 * BLK)
        first = base + (8 + place) * BLK
        self.q_pos = lax.broadcasted_iota(jnp.int32, (1, BLK), 1) + (8 + place) * BLK
        starts = jnp.zeros((1, BLK), jnp.int32) - base
        first_start = -base
        last_start = -base
        end = jnp.int32(0)
        for c in range(16):
            end = end + len_ref[c]
            rel = end - base
            starts = jnp.where(self.q_pos >= rel, rel, starts)
            first_start = jnp.where(end <= first, rel, first_start)
            last_start = jnp.where(end <= first + BLK - 1, rel, last_start)
        self.starts = starts
        self.last_start = last_start
        self.lo = first_start // BLK
        self.hi = 8 + place

    def slot(self, j, dz, dc):
        return (2 - j) * 4 + (1 - self.zh if dz else self.zh) * 2 + (1 - self.core if dc else self.core)

    def mask(self, t):
        k_pos = lax.broadcasted_iota(jnp.int32, (BLK, BLK), 0) + t * BLK
        return (k_pos >= self.starts) & (k_pos <= self.q_pos)


def attention_kernel(*refs):
    len_ref, q_ref, do_ref = refs[:3]
    kv_refs = refs[3:15]
    o_ref, dq_ref = refs[15:17]
    out_refs = refs[17:21]
    kvs, dkvs, qt, dot_t, do_s, probs, row_max, total, acc, dq_acc, stage, delta, norms, in_sem, out_sem = refs[21:]
    at = Place(len_ref)
    order = [(j, dz, dc) for j in range(ROWS) for dz, dc in NEAR]
    for n, where in enumerate(order):
        slot = at.slot(*where)
        pltpu.make_async_copy(kv_refs[n], kvs.at[slot], in_sem.at[slot]).start()

    def arrived(t):
        pltpu.make_async_copy(kv_refs[0], kvs.at[t], in_sem.at[t]).wait()

    def out_copy(n, part, t):
        j, dz, dc = order[n]
        return pltpu.make_async_copy(dkvs.at[t, part], out_refs[part * 2 + dc].at[j, dz], out_sem.at[n, part])

    begin, end = at.lo, at.hi + 1
    dkvs[SLOTS] = jnp.zeros((2, BLK, HD), BF16)
    for n, where in enumerate(order):
        slot = at.slot(*where)

        @pl.when((slot < begin) | (slot >= end))
        def _():
            for part in range(2):
                out_copy(n, part, SLOTS).start()

    for h in range(HEADS):
        cols = slice(h * BLK, (h + 1) * BLK)
        qt[:, cols] = q_ref[h].T
        dot_t[:, cols] = do_ref[h].T
    dq_acc[...] = jnp.zeros((HD, NQ), F32)
    norms[...] = jnp.zeros((8, HD), F32)

    def forward(t, masked, shift):
        k = kvs[t, 0]
        v_t = kvs[t, 1].T
        if not shift:
            squares = dot(jnp.square(k.astype(F32)).astype(BF16), jnp.ones((HD, HD), BF16))
            norms[...] = jnp.maximum(norms[...], jnp.max(squares.reshape(BLK // 8, 8, HD), axis=0))
        if masked:
            allowed = at.mask(t)

        def score(h):
            s = dot(k, qt[:, h * HALF:(h + 1) * HALF])
            return jnp.where(allowed[:, (h % 2) * HALF:(h % 2 + 1) * HALF], s, NEGATIVE) if masked else s

        def soft(h, s):
            cols = slice(h * HALF, (h + 1) * HALF)
            p = jnp.exp2(s * LOG2 - row_max[:, cols] if shift else s * LOG2)
            total[:, cols] += jnp.sum(p, axis=0, keepdims=True)
            p = p.astype(BF16)
            probs[t - begin, :, cols] = p
            return p

        def product(h, p):
            acc[:, h * HALF:(h + 1) * HALF] += dot(v_t, p)

        weights = soft(0, score(0))
        s = score(1)
        for h in range(1, 2 * HEADS):
            held, weights = weights, soft(h, s)
            if h + 1 < 2 * HEADS:
                s = score(h + 1)
            product(h - 1, held)
        product(2 * HEADS - 1, weights)

    def clear():
        total[...] = jnp.zeros((1, NQ), F32)
        acc[...] = jnp.zeros((HD, NQ), F32)

    def fast_step(t, carry):
        arrived(t)
        masked = (t * BLK < at.last_start) | (t == at.hi)

        @pl.when(masked)
        def _():
            forward(t, True, False)

        @pl.when(jnp.logical_not(masked))
        def _():
            forward(t, False, False)

        return carry

    def max_step(t, carry):
        allowed = at.mask(t)
        for h in range(HEADS):
            cols = slice(h * BLK, (h + 1) * BLK)
            s = jnp.where(allowed, dot(kvs[t, 0], qt[:, cols]), NEGATIVE)
            row_max[:, cols] = jnp.maximum(row_max[:, cols], jnp.max(s, axis=0, keepdims=True))
        return carry

    def slow_step(t, carry):
        forward(t, True, True)
        return carry

    clear()
    lax.fori_loop(begin, end, fast_step, 0)
    q_norm = jnp.max(dot(jnp.ones((8, HD), BF16), jnp.square(qt[...].astype(F32)).astype(BF16)))

    @pl.when(q_norm * jnp.max(norms[...]) > 0.98 * (BOUND / LOG2) ** 2)
    def _():
        clear()
        row_max[...] = jnp.full((1, NQ), NEGATIVE, F32)
        lax.fori_loop(begin, end, max_step, 0)
        row_max[...] = row_max[...] * LOG2
        lax.fori_loop(begin, end, slow_step, 0)

    for h in range(HEADS):
        cols = slice(h * BLK, (h + 1) * BLK)
        inverse = 1.0 / total[:, cols]
        o = (acc[:, cols] * inverse).astype(BF16)
        o_ref[h] = o.T
        scaled = (dot_t[:, cols].astype(F32) * inverse).astype(BF16)
        dot_t[:, cols] = scaled
        do_s[h * BLK:(h + 1) * BLK] = scaled.T
        delta[:, cols] = jnp.sum(o.astype(F32) * scaled.astype(F32), axis=0, keepdims=True)

    def backward_step(t, carry):
        k_t = kvs[t, 0].T
        v = kvs[t, 1]

        def dp_of(h):
            return dot(v, dot_t[:, h * BLK:(h + 1) * BLK])

        def ds_of(h, dp):
            cols = slice(h * BLK, (h + 1) * BLK)
            ds = (probs[t - begin, :, cols].astype(F32) * (dp - delta[:, cols])).astype(BF16)
            stage[:, cols] = ds
            return ds

        def dq_of(h, ds):
            dq_acc[:, h * BLK:(h + 1) * BLK] += dot(k_t, ds)

        d0 = dp_of(0)
        d1 = dp_of(1)
        s0 = ds_of(0, d0)
        dkvs[t, 1] = dot(probs[t - begin], do_s[...]).astype(BF16)
        d2 = dp_of(2)
        dq_of(0, s0)
        s1 = ds_of(1, d1)
        d3 = dp_of(3)
        dq_of(1, s1)
        s2 = ds_of(2, d2)
        dq_of(2, s2)
        s3 = ds_of(3, d3)
        dq_of(3, s3)
        dkvs[t, 0] = (dot(stage[...], q_ref[...].reshape(NQ, HD)) * SCALE).astype(BF16)

        for n, where in enumerate(order):
            @pl.when(at.slot(*where) == t)
            def _():
                for part in range(2):
                    out_copy(n, part, t).start()

        return carry

    lax.fori_loop(begin, end, backward_step, 0)
    for h in range(HEADS):
        dq_ref[h] = (dq_acc[:, h * BLK:(h + 1) * BLK] * SCALE).astype(BF16).T

    def rest(t, carry):
        arrived(t)
        return carry

    lax.fori_loop(0, begin, rest, 0)
    lax.fori_loop(end, SLOTS, rest, 0)
    for n in range(len(order)):
        for part in range(2):
            out_copy(n, part, 0).wait()


def attention(seq_lengths, queries, d_out, blocks):
    rows = shape((HEADS, BLK, HD), BF16)
    grads = shape((ROWS, 2, BLK, HD), BF16)
    return pl.pallas_call(
        attention_kernel,
        out_shape=(rows, rows) + (grads,) * 4,
        in_specs=[SMEM, VMEM, VMEM] + [ANY] * SLOTS,
        out_specs=[VMEM, VMEM] + [ANY] * 4,
        scratch_shapes=[
            pltpu.VMEM((SLOTS, 2, BLK, HD), BF16),
            pltpu.VMEM((SLOTS + 1, 2, BLK, HD), BF16),
            pltpu.VMEM((HD, NQ), BF16),
            pltpu.VMEM((HD, NQ), BF16),
            pltpu.VMEM((NQ, HD), BF16),
            pltpu.VMEM((SPAN, BLK, NQ), BF16),
            pltpu.VMEM((1, NQ), F32),
            pltpu.VMEM((1, NQ), F32),
            pltpu.VMEM((HD, NQ), F32),
            pltpu.VMEM((HD, NQ), F32),
            pltpu.VMEM((BLK, NQ), BF16),
            pltpu.VMEM((1, NQ), F32),
            pltpu.VMEM((8, HD), F32),
            DMA((SLOTS,)),
            DMA((SLOTS, 2)),
        ],
        compiler_params=pltpu.CompilerParams(vmem_limit_bytes=56 << 20),
        cost_estimate=pl.CostEstimate(flops=8 << 30, bytes_accessed=16 << 20, transcendentals=9 << 20),
        name="attention",
    )(seq_lengths, queries, d_out, *blocks)


def swap_core(value):
    return lax.ppermute(value, "core", [(0, 1), (1, 0)])


def swap_z(value, sources=(0, 1)):
    pairs = [(2 * zh + zl, 2 * (1 - zh) + (1 - zl)) for zh in sources for zl in range(2)]
    return lax.ppermute(value, ("zh", "zl"), pairs)


def swap_head(value):
    return lax.ppermute(value, "zl", [(0, 1), (1, 0)])


def shift_row(value, by):
    return lax.ppermute(value, ("x", "y"), [(r, (r + by) % 16) for r in range(16)])


def added(*values):
    total = values[0].astype(F32)
    for value in values[1:]:
        total = total + value.astype(F32)
    return total.astype(BF16)


def returned(keep, send):
    first = lax.axis_index("zh") == 0
    zero = jnp.zeros((), BF16)
    given = [swap_core(part) for part in send]
    outer, middle = [], []
    for a, b in zip(keep, given):
        outer.append(added(jnp.where(first, a[2, 1], a[0, 1]), jnp.where(first, b[2, 1], b[0, 1])))
        middle.append(added(a[1, 1], b[1, 1]))
    outer = [swap_z(value) for value in outer]
    middle = [swap_z(lax.optimization_barrier(both)[0]) for both in zip(middle, outer)]
    done = []
    for a, b, far, near in zip(keep, given, outer, middle):
        back = shift_row(added(a[2, 0], b[2, 0], jnp.where(first, zero, far)), -1)
        back = shift_row(added(a[1, 0], b[1, 0], near, back), -1)
        done.append(added(a[0, 0], b[0, 0], jnp.where(first, far, zero), back))
    return [added(half, swap_head(half)) for half in done]


def on_device(queries, key_rows, value_rows, d_out, seq_lengths):
    own = jnp.stack([key_rows, value_rows])
    row1 = shift_row(own, 1)
    side0 = swap_z(own, (0,))
    row2 = shift_row(row1, 1)
    side1 = swap_z(lax.optimization_barrier((row1, side0))[0])
    side2 = swap_z(row2, (1,))
    blocks = []
    for block in (own, side0, row1, side1, row2, side2):
        blocks += [block, swap_core(block)]
    attended, grad_queries, *parts = attention(seq_lengths, queries, d_out, blocks)
    grad_keys, grad_values = returned(parts[::2], parts[1::2])
    return attended, grad_queries, grad_keys, grad_values


def solution(mesh):
    fine = Mesh(mesh.devices.reshape(4, 4, 2, 2, 2), ("x", "y", "zh", "core", "zl"))
    tokens = P("zl", SEQ, None)
    rows = P(SEQ, None)
    return jax.shard_map(
        on_device,
        mesh=fine,
        in_specs=(tokens, rows, rows, tokens, P()),
        out_specs=(tokens, tokens, rows, rows),
        check_vma=False,
    )
```

```python
import math

import jax
import jax.numpy as jnp
from jax import lax
from jax.experimental import pallas as pl
from jax.experimental.pallas import tpu as pltpu
from jax.sharding import Mesh, PartitionSpec as P

NEGATIVE = -1e30
BLK = 512
HEADS = 4
HD = 128
NQ = HEADS * BLK
HALF = BLK // 2
ROWS = 3
SLOTS = 4 * ROWS
GROUP = 3
SPAN = 9
SCALE = HD ** -0.5
LOG2 = SCALE * math.log2(math.e)
BOUND = 64.0
F32 = jnp.float32
BF16 = jnp.bfloat16
SEQ = ("x", "y", "zh", "core")
VMEM = pl.BlockSpec(memory_space=pltpu.VMEM)
SMEM = pl.BlockSpec(memory_space=pltpu.SMEM)
ANY = pl.BlockSpec(memory_space=pl.ANY)
DMA = pltpu.SemaphoreType.DMA
NEAR = [(dz, dc) for dz in range(2) for dc in range(2)]


def shape(dims, dtype):
    return jax.ShapeDtypeStruct(dims, dtype)


def dot(a, b):
    return lax.dot_general(a, b, (((1,), (0,)), ((), ())), preferred_element_type=F32)


class Place:
    def __init__(self, len_ref):
        row = lax.axis_index("x") * 4 + lax.axis_index("y")
        self.zh = lax.axis_index("zh")
        self.core = lax.axis_index("core")
        place = self.zh * 2 + self.core
        base = (row - 2) * (4 * BLK)
        first = base + (8 + place) * BLK
        self.q_pos = lax.broadcasted_iota(jnp.int32, (1, BLK), 1) + (8 + place) * BLK
        starts = jnp.zeros((1, BLK), jnp.int32) - base
        first_start = -base
        last_start = -base
        end = jnp.int32(0)
        for c in range(16):
            end = end + len_ref[c]
            rel = end - base
            starts = jnp.where(self.q_pos >= rel, rel, starts)
            first_start = jnp.where(end <= first, rel, first_start)
            last_start = jnp.where(end <= first + BLK - 1, rel, last_start)
        self.starts = starts
        self.last_start = last_start
        self.lo = first_start // BLK
        self.hi = 8 + place

    def slot(self, j, dz, dc):
        return (2 - j) * 4 + (1 - self.zh if dz else self.zh) * 2 + (1 - self.core if dc else self.core)

    def mask(self, t):
        k_pos = lax.broadcasted_iota(jnp.int32, (BLK, BLK), 0) + t * BLK
        return (k_pos >= self.starts) & (k_pos <= self.q_pos)


def attention_kernel(*refs):
    len_ref, q_hbm, do_hbm = refs[:3]
    kv_refs = refs[3:15]
    o_hbm, dq_hbm = refs[15:17]
    out_refs = refs[17:21]
    kvs, dkvs, qt, dot_t, do_s, probs, row_max, total, acc, dq_acc, stage, delta, norms, q_ref, do_ref, o_ref, dq_ref, row_sem, in_sem, out_sem = refs[21:]
    loads = [[pltpu.make_async_copy(a.at[h], b.at[h], row_sem.at[n, h]) for n, (a, b) in enumerate(((q_hbm, q_ref), (do_hbm, do_ref)))] for h in range(HEADS)]
    for pair in loads:
        for copy in pair:
            copy.start()
    at = Place(len_ref)
    order = [(j, dz, dc) for j in range(ROWS) for dz, dc in NEAR]
    for n, where in enumerate(order):
        slot = at.slot(*where)
        pltpu.make_async_copy(kv_refs[n], kvs.at[slot], in_sem.at[slot]).start()

    def arrived(t):
        pltpu.make_async_copy(kv_refs[0], kvs.at[t], in_sem.at[t]).wait()

    def out_copy(n, part, t):
        j, dz, dc = order[n]
        return pltpu.make_async_copy(dkvs.at[t, part], out_refs[part * 2 + dc].at[j, dz], out_sem.at[n, part])

    begin = at.lo
    end = begin + (at.hi - begin + GROUP) // GROUP * GROUP
    for spare in range(SLOTS, SLOTS + GROUP - 1):
        kvs[spare] = jnp.zeros((2, BLK, HD), BF16)
    dkvs[SLOTS + GROUP - 1] = jnp.zeros((2, BLK, HD), BF16)
    for n, where in enumerate(order):
        slot = at.slot(*where)

        @pl.when((slot < begin) | (slot >= end))
        def _():
            for part in range(2):
                out_copy(n, part, SLOTS + GROUP - 1).start()

    for h in range(HEADS):
        cols = slice(h * BLK, (h + 1) * BLK)
        for copy in loads[h]:
            copy.wait()
        qt[:, cols] = q_ref[h].T
        dot_t[:, cols] = do_ref[h].T
    dq_acc[...] = jnp.zeros((HD, NQ), F32)
    norms[...] = jnp.zeros((8, HD), F32)

    def forward(t, masked, shift):
        k = kvs[t, 0]
        v_t = kvs[t, 1].T
        if not shift:
            squares = dot(jnp.square(k.astype(F32)).astype(BF16), jnp.ones((HD, HD), BF16))
            norms[...] = jnp.maximum(norms[...], jnp.max(squares.reshape(BLK // 8, 8, HD), axis=0))
        if masked:
            allowed = at.mask(t)

        def score(h):
            s = dot(k, qt[:, h * HALF:(h + 1) * HALF])
            return jnp.where(allowed[:, (h % 2) * HALF:(h % 2 + 1) * HALF], s, NEGATIVE) if masked else s

        def soft(h, s):
            cols = slice(h * HALF, (h + 1) * HALF)
            p = jnp.exp2(s * LOG2 - row_max[:, cols] if shift else s * LOG2)
            total[:, cols] += jnp.sum(p, axis=0, keepdims=True)
            p = p.astype(BF16)
            probs[t - begin, :, cols] = p
            return p

        def product(h, p):
            acc[:, h * HALF:(h + 1) * HALF] += dot(v_t, p)

        weights = soft(0, score(0))
        s = score(1)
        for h in range(1, 2 * HEADS):
            held, weights = weights, soft(h, s)
            if h + 1 < 2 * HEADS:
                s = score(h + 1)
            product(h - 1, held)
        product(2 * HEADS - 1, weights)

    def clear():
        total[...] = jnp.zeros((1, NQ), F32)
        acc[...] = jnp.zeros((HD, NQ), F32)

    def fast_step(i, carry):
        for u in range(GROUP):
            t = begin + i * GROUP + u

            @pl.when(t < SLOTS)
            def _():
                arrived(t)

        for u in range(GROUP):
            forward(begin + i * GROUP + u, True, False)

        return carry

    def max_step(t, carry):
        allowed = at.mask(t)
        for h in range(HEADS):
            cols = slice(h * BLK, (h + 1) * BLK)
            s = jnp.where(allowed, dot(kvs[t, 0], qt[:, cols]), NEGATIVE)
            row_max[:, cols] = jnp.maximum(row_max[:, cols], jnp.max(s, axis=0, keepdims=True))
        return carry

    def slow_step(t, carry):
        forward(t, True, True)
        return carry

    clear()
    lax.fori_loop(0, (end - begin) // GROUP, fast_step, 0)
    q_norm = jnp.max(dot(jnp.ones((8, HD), BF16), jnp.square(qt[...].astype(F32)).astype(BF16)))

    @pl.when(q_norm * jnp.max(norms[...]) > 0.98 * (BOUND / LOG2) ** 2)
    def _():
        clear()
        row_max[...] = jnp.full((1, NQ), NEGATIVE, F32)
        lax.fori_loop(begin, end, max_step, 0)
        row_max[...] = row_max[...] * LOG2
        lax.fori_loop(begin, end, slow_step, 0)

    for h in range(HEADS):
        cols = slice(h * BLK, (h + 1) * BLK)
        inverse = 1.0 / total[:, cols]
        o = (acc[:, cols] * inverse).astype(BF16)
        o_ref[h] = o.T
        pltpu.make_async_copy(o_ref.at[h], o_hbm.at[h], row_sem.at[2, h]).start()
        scaled = (dot_t[:, cols].astype(F32) * inverse).astype(BF16)
        dot_t[:, cols] = scaled
        do_s[h * BLK:(h + 1) * BLK] = scaled.T
        delta[:, cols] = jnp.sum(o.astype(F32) * scaled.astype(F32), axis=0, keepdims=True)

    def backward_tile(t, u):
        v = kvs[t, 1]

        def dp_of(h):
            return dot(v, dot_t[:, h * BLK:(h + 1) * BLK])

        def ds_of(h, dp):
            cols = slice(h * BLK, (h + 1) * BLK)
            ds = (probs[t - begin, :, cols].astype(F32) * (dp - delta[:, cols])).astype(BF16)
            stage[u * BLK:(u + 1) * BLK, cols] = ds
            return ds

        d0 = dp_of(0)
        d1 = dp_of(1)
        ds_of(0, d0)
        dkvs[t, 1] = dot(probs[t - begin], do_s[...]).astype(BF16)
        d2 = dp_of(2)
        ds_of(1, d1)
        d3 = dp_of(3)
        ds_of(2, d2)
        ds_of(3, d3)
        dkvs[t, 0] = (dot(stage[u * BLK:(u + 1) * BLK], q_ref[...].reshape(NQ, HD)) * SCALE).astype(BF16)

    def backward_step(i, carry):
        first = begin + i * GROUP
        for u in range(GROUP):
            backward_tile(first + u, u)
        k_t = jnp.concatenate([kvs[first + u, 0].T for u in range(GROUP)], axis=1)
        for h in range(HEADS):
            cols = slice(h * BLK, (h + 1) * BLK)
            dq_acc[:, cols] += dot(k_t, stage[:, cols])
        for n, where in enumerate(order):
            slot = at.slot(*where)

            @pl.when((slot >= first) & (slot < first + GROUP))
            def _():
                for part in range(2):
                    out_copy(n, part, slot).start()

        return carry

    lax.fori_loop(0, (end - begin) // GROUP, backward_step, 0)
    for h in range(HEADS):
        dq_ref[h] = (dq_acc[:, h * BLK:(h + 1) * BLK] * SCALE).astype(BF16).T
        pltpu.make_async_copy(dq_ref.at[h], dq_hbm.at[h], row_sem.at[3, h]).start()

    def rest(t, carry):
        arrived(t)
        return carry

    lax.fori_loop(0, begin, rest, 0)
    lax.fori_loop(jnp.minimum(end, SLOTS), SLOTS, rest, 0)
    for n in range(len(order)):
        for part in range(2):
            out_copy(n, part, 0).wait()
    for h in range(HEADS):
        pltpu.make_async_copy(o_ref.at[h], o_hbm.at[h], row_sem.at[2, h]).wait()
        pltpu.make_async_copy(dq_ref.at[h], dq_hbm.at[h], row_sem.at[3, h]).wait()


def attention(seq_lengths, queries, d_out, blocks):
    rows = shape((HEADS, BLK, HD), BF16)
    grads = shape((ROWS, 2, BLK, HD), BF16)
    return pl.pallas_call(
        attention_kernel,
        out_shape=(rows, rows) + (grads,) * 4,
        in_specs=[SMEM] + [ANY] * (2 + SLOTS),
        out_specs=[ANY] * 6,
        scratch_shapes=[
            pltpu.VMEM((SLOTS + GROUP - 1, 2, BLK, HD), BF16),
            pltpu.VMEM((SLOTS + GROUP, 2, BLK, HD), BF16),
            pltpu.VMEM((HD, NQ), BF16),
            pltpu.VMEM((HD, NQ), BF16),
            pltpu.VMEM((NQ, HD), BF16),
            pltpu.VMEM((SPAN, BLK, NQ), BF16),
            pltpu.VMEM((1, NQ), F32),
            pltpu.VMEM((1, NQ), F32),
            pltpu.VMEM((HD, NQ), F32),
            pltpu.VMEM((HD, NQ), F32),
            pltpu.VMEM((GROUP * BLK, NQ), BF16),
            pltpu.VMEM((1, NQ), F32),
            pltpu.VMEM((8, HD), F32),
            pltpu.VMEM((HEADS, BLK, HD), BF16),
            pltpu.VMEM((HEADS, BLK, HD), BF16),
            pltpu.VMEM((HEADS, BLK, HD), BF16),
            pltpu.VMEM((HEADS, BLK, HD), BF16),
            DMA((4, HEADS)),
            DMA((SLOTS,)),
            DMA((SLOTS, 2)),
        ],
        compiler_params=pltpu.CompilerParams(vmem_limit_bytes=56 << 20),
        cost_estimate=pl.CostEstimate(flops=8 << 30, bytes_accessed=16 << 20, transcendentals=9 << 20),
        name="attention",
    )(seq_lengths, queries, d_out, *blocks)


def swap_core(value):
    return lax.ppermute(value, "core", [(0, 1), (1, 0)])


def swap_z(value, sources=(0, 1)):
    pairs = [(2 * zh + zl, 2 * (1 - zh) + (1 - zl)) for zh in sources for zl in range(2)]
    return lax.ppermute(value, ("zh", "zl"), pairs)


def swap_head(value):
    return lax.ppermute(value, "zl", [(0, 1), (1, 0)])


def shift_row(value, by):
    return lax.ppermute(value, ("x", "y"), [(r, (r + by) % 16) for r in range(16)])


def added(*values):
    total = values[0].astype(F32)
    for value in values[1:]:
        total = total + value.astype(F32)
    return total.astype(BF16)


def returned(keep, send):
    first = lax.axis_index("zh") == 0
    zero = jnp.zeros((), BF16)
    given = [swap_core(part) for part in send]
    outer, middle = [], []
    for a, b in zip(keep, given):
        outer.append(added(jnp.where(first, a[2, 1], a[0, 1]), jnp.where(first, b[2, 1], b[0, 1])))
        middle.append(added(a[1, 1], b[1, 1]))
    outer = [swap_z(value) for value in outer]
    middle = [swap_z(lax.optimization_barrier(both)[0]) for both in zip(middle, outer)]
    done = []
    for a, b, far, near in zip(keep, given, outer, middle):
        back = shift_row(added(a[2, 0], b[2, 0], jnp.where(first, zero, far)), -1)
        back = shift_row(added(a[1, 0], b[1, 0], near, back), -1)
        done.append(added(a[0, 0], b[0, 0], jnp.where(first, far, zero), back))
    return [added(half, swap_head(half)) for half in done]


def on_device(queries, key_rows, value_rows, d_out, seq_lengths):
    own = jnp.stack([key_rows, value_rows])
    row1 = shift_row(own, 1)
    side0 = swap_z(own, (0,))
    row2 = shift_row(row1, 1)
    side1 = swap_z(lax.optimization_barrier((row1, side0))[0])
    side2 = swap_z(row2, (1,))
    blocks = []
    for block in (own, side0, row1, side1, row2, side2):
        blocks += [block, swap_core(block)]
    attended, grad_queries, *parts = attention(seq_lengths, queries, d_out, blocks)
    grad_keys, grad_values = returned(parts[::2], parts[1::2])
    return attended, grad_queries, grad_keys, grad_values


def solution(mesh):
    fine = Mesh(mesh.devices.reshape(4, 4, 2, 2, 2), ("x", "y", "zh", "core", "zl"))
    tokens = P("zl", SEQ, None)
    rows = P(SEQ, None)
    return jax.shard_map(
        on_device,
        mesh=fine,
        in_specs=(tokens, rows, rows, tokens, P()),
        out_specs=(tokens, tokens, rows, rows),
        check_vma=False,
    )
```

```python
import math

import jax
import jax.numpy as jnp
from jax import lax
from jax.experimental import pallas as pl
from jax.experimental.pallas import tpu as pltpu
from jax.sharding import Mesh, PartitionSpec as P

NEGATIVE = -1e30
BLK = 512
HEADS = 4
HD = 128
NQ = HEADS * BLK
HALF = BLK // 2
ROWS = 3
SLOTS = 4 * ROWS
GROUP = 3
SPAN = 9
SCALE = HD ** -0.5
LOG2 = SCALE * math.log2(math.e)
BOUND = 64.0
F32 = jnp.float32
BF16 = jnp.bfloat16
SEQ = ("x", "y", "zh", "core")
VMEM = pl.BlockSpec(memory_space=pltpu.VMEM)
SMEM = pl.BlockSpec(memory_space=pltpu.SMEM)
ANY = pl.BlockSpec(memory_space=pl.ANY)
DMA = pltpu.SemaphoreType.DMA
NEAR = [(dz, dc) for dz in range(2) for dc in range(2)]


def shape(dims, dtype):
    return jax.ShapeDtypeStruct(dims, dtype)


def dot(a, b):
    return lax.dot_general(a, b, (((1,), (0,)), ((), ())), preferred_element_type=F32)


class Place:
    def __init__(self, len_ref):
        row = lax.axis_index("x") * 4 + lax.axis_index("y")
        self.zh = lax.axis_index("zh")
        self.core = lax.axis_index("core")
        place = self.zh * 2 + self.core
        base = (row - 2) * (4 * BLK)
        first = base + (8 + place) * BLK
        self.q_pos = lax.broadcasted_iota(jnp.int32, (1, BLK), 1) + (8 + place) * BLK
        starts = jnp.zeros((1, BLK), jnp.int32) - base
        first_start = -base
        last_start = -base
        end = jnp.int32(0)
        for c in range(16):
            end = end + len_ref[c]
            rel = end - base
            starts = jnp.where(self.q_pos >= rel, rel, starts)
            first_start = jnp.where(end <= first, rel, first_start)
            last_start = jnp.where(end <= first + BLK - 1, rel, last_start)
        self.starts = starts
        self.last_start = last_start
        self.lo = first_start // BLK
        self.hi = 8 + place

    def slot(self, j, dz, dc):
        return (2 - j) * 4 + (1 - self.zh if dz else self.zh) * 2 + (1 - self.core if dc else self.core)

    def mask(self, t):
        k_pos = lax.broadcasted_iota(jnp.int32, (BLK, BLK), 0) + t * BLK
        return (k_pos >= self.starts) & (k_pos <= self.q_pos)


def attention_kernel(*refs):
    len_ref, q_hbm, do_hbm = refs[:3]
    kv_refs = refs[3:15]
    o_hbm, dq_hbm = refs[15:17]
    out_refs = refs[17:21]
    kvs, dkvs, qt, dot_t, do_s, probs, row_max, total, acc, dq_acc, stage, delta, norms, q_ref, do_ref, o_ref, dq_ref, row_sem, in_sem, out_sem = refs[21:]
    loads = [[pltpu.make_async_copy(a.at[h], b.at[h], row_sem.at[n, h]) for n, (a, b) in enumerate(((q_hbm, q_ref), (do_hbm, do_ref)))] for h in range(HEADS)]
    for pair in loads:
        for copy in pair:
            copy.start()
    at = Place(len_ref)
    order = [(j, dz, dc) for j in range(ROWS) for dz, dc in NEAR]
    for n, where in enumerate(order):
        slot = at.slot(*where)
        pltpu.make_async_copy(kv_refs[n], kvs.at[slot], in_sem.at[slot]).start()

    def arrived(t):
        pltpu.make_async_copy(kv_refs[0], kvs.at[t], in_sem.at[t]).wait()

    def out_copy(n, part, t):
        j, dz, dc = order[n]
        return pltpu.make_async_copy(dkvs.at[t, part], out_refs[part * 2 + dc].at[j, dz], out_sem.at[n, part])

    begin = at.lo
    end = begin + (at.hi - begin + GROUP) // GROUP * GROUP
    for spare in range(SLOTS, SLOTS + GROUP - 1):
        kvs[spare] = jnp.zeros((2, BLK, HD), BF16)
    dkvs[SLOTS + GROUP - 1] = jnp.zeros((2, BLK, HD), BF16)
    for n, where in enumerate(order):
        slot = at.slot(*where)

        @pl.when((slot < begin) | (slot >= end))
        def _():
            for part in range(2):
                out_copy(n, part, SLOTS + GROUP - 1).start()

    for h in range(HEADS):
        cols = slice(h * BLK, (h + 1) * BLK)
        for copy in loads[h]:
            copy.wait()
        qt[:, cols] = q_ref[h].T
        dot_t[:, cols] = do_ref[h].T
    dq_acc[...] = jnp.zeros((HD, NQ), F32)
    norms[...] = jnp.zeros((8, HD), F32)

    def forward(t, masked, shift):
        k = kvs[t, 0]
        v_t = kvs[t, 1].T
        if not shift:
            squares = dot(jnp.square(k.astype(F32)).astype(BF16), jnp.ones((HD, HD), BF16))
            norms[...] = jnp.maximum(norms[...], jnp.max(squares.reshape(BLK // 8, 8, HD), axis=0))
        if masked:
            allowed = at.mask(t)

        def score(h):
            s = dot(k, qt[:, h * HALF:(h + 1) * HALF])
            return jnp.where(allowed[:, (h % 2) * HALF:(h % 2 + 1) * HALF], s, NEGATIVE) if masked else s

        def soft(h, s):
            cols = slice(h * HALF, (h + 1) * HALF)
            p = jnp.exp2(s * LOG2 - row_max[:, cols] if shift else s * LOG2)
            total[:, cols] += jnp.sum(p, axis=0, keepdims=True)
            p = p.astype(BF16)
            probs[t - begin, :, cols] = p
            return p

        def product(h, p):
            acc[:, h * HALF:(h + 1) * HALF] += dot(v_t, p)

        weights = soft(0, score(0))
        s = score(1)
        for h in range(1, 2 * HEADS):
            held, weights = weights, soft(h, s)
            if h + 1 < 2 * HEADS:
                s = score(h + 1)
            product(h - 1, held)
        product(2 * HEADS - 1, weights)

    def clear():
        total[...] = jnp.zeros((1, NQ), F32)
        acc[...] = jnp.zeros((HD, NQ), F32)

    def fast_step(i, carry):
        for u in range(GROUP):
            t = begin + i * GROUP + u

            @pl.when(t < SLOTS)
            def _():
                arrived(t)

        for u in range(GROUP):
            forward(begin + i * GROUP + u, True, False)

        return carry

    def max_step(t, carry):
        allowed = at.mask(t)
        for h in range(HEADS):
            cols = slice(h * BLK, (h + 1) * BLK)
            s = jnp.where(allowed, dot(kvs[t, 0], qt[:, cols]), NEGATIVE)
            row_max[:, cols] = jnp.maximum(row_max[:, cols], jnp.max(s, axis=0, keepdims=True))
        return carry

    def slow_step(t, carry):
        forward(t, True, True)
        return carry

    clear()
    lax.fori_loop(0, (end - begin) // GROUP, fast_step, 0)
    q_norm = jnp.max(dot(jnp.ones((8, HD), BF16), jnp.square(qt[...].astype(F32)).astype(BF16)))

    @pl.when(q_norm * jnp.max(norms[...]) > 0.98 * (BOUND / LOG2) ** 2)
    def _():
        clear()
        row_max[...] = jnp.full((1, NQ), NEGATIVE, F32)
        lax.fori_loop(begin, end, max_step, 0)
        row_max[...] = row_max[...] * LOG2
        lax.fori_loop(begin, end, slow_step, 0)

    for h in range(HEADS):
        cols = slice(h * BLK, (h + 1) * BLK)
        inverse = 1.0 / total[:, cols]
        o = (acc[:, cols] * inverse).astype(BF16)
        o_ref[h] = o.T
        pltpu.make_async_copy(o_ref.at[h], o_hbm.at[h], row_sem.at[2, h]).start()
        scaled = (dot_t[:, cols].astype(F32) * inverse).astype(BF16)
        dot_t[:, cols] = scaled
        do_s[h * BLK:(h + 1) * BLK] = scaled.T
        delta[:, cols] = jnp.sum(o.astype(F32) * scaled.astype(F32), axis=0, keepdims=True)

    def backward_tile(t, u):
        v = kvs[t, 1]

        def dp_of(h):
            return dot(v, dot_t[:, h * BLK:(h + 1) * BLK])

        def ds_of(h, dp):
            cols = slice(h * BLK, (h + 1) * BLK)
            ds = (probs[t - begin, :, cols].astype(F32) * (dp - delta[:, cols])).astype(BF16)
            stage[u * BLK:(u + 1) * BLK, cols] = ds
            return ds

        d0 = dp_of(0)
        d1 = dp_of(1)
        ds_of(0, d0)
        dkvs[t, 1] = dot(probs[t - begin], do_s[...]).astype(BF16)
        d2 = dp_of(2)
        ds_of(1, d1)
        d3 = dp_of(3)
        ds_of(2, d2)
        ds_of(3, d3)
        dkvs[t, 0] = (dot(stage[u * BLK:(u + 1) * BLK], q_ref[...].reshape(NQ, HD)) * SCALE).astype(BF16)

    def backward_step(i, carry):
        first = begin + i * GROUP
        for u in range(GROUP):
            backward_tile(first + u, u)
        k_t = jnp.concatenate([kvs[first + u, 0].T for u in range(GROUP)], axis=1)
        for h in range(HEADS):
            cols = slice(h * BLK, (h + 1) * BLK)
            dq_acc[:, cols] += dot(k_t, stage[:, cols])
        for n, where in enumerate(order):
            slot = at.slot(*where)

            @pl.when((slot >= first) & (slot < first + GROUP))
            def _():
                for part in range(2):
                    out_copy(n, part, slot).start()

        return carry

    lax.fori_loop(0, (end - begin) // GROUP, backward_step, 0)
    for h in range(HEADS):
        dq_ref[h] = (dq_acc[:, h * BLK:(h + 1) * BLK] * SCALE).astype(BF16).T
        pltpu.make_async_copy(dq_ref.at[h], dq_hbm.at[h], row_sem.at[3, h]).start()

    def rest(t, carry):
        arrived(t)
        return carry

    lax.fori_loop(0, begin, rest, 0)
    lax.fori_loop(jnp.minimum(end, SLOTS), SLOTS, rest, 0)
    for n in range(len(order)):
        for part in range(2):
            out_copy(n, part, 0).wait()
    for h in range(HEADS):
        pltpu.make_async_copy(o_ref.at[h], o_hbm.at[h], row_sem.at[2, h]).wait()
        pltpu.make_async_copy(dq_ref.at[h], dq_hbm.at[h], row_sem.at[3, h]).wait()


def attention(seq_lengths, queries, d_out, blocks):
    rows = shape((HEADS, BLK, HD), BF16)
    grads = shape((ROWS, 2, BLK, HD), BF16)
    return pl.pallas_call(
        attention_kernel,
        out_shape=(rows, rows) + (grads,) * 4,
        in_specs=[SMEM] + [ANY] * (2 + SLOTS),
        out_specs=[ANY] * 6,
        scratch_shapes=[
            pltpu.VMEM((SLOTS + GROUP - 1, 2, BLK, HD), BF16),
            pltpu.VMEM((SLOTS + GROUP, 2, BLK, HD), BF16),
            pltpu.VMEM((HD, NQ), BF16),
            pltpu.VMEM((HD, NQ), BF16),
            pltpu.VMEM((NQ, HD), BF16),
            pltpu.VMEM((SPAN, BLK, NQ), BF16),
            pltpu.VMEM((1, NQ), F32),
            pltpu.VMEM((1, NQ), F32),
            pltpu.VMEM((HD, NQ), F32),
            pltpu.VMEM((HD, NQ), F32),
            pltpu.VMEM((GROUP * BLK, NQ), BF16),
            pltpu.VMEM((1, NQ), F32),
            pltpu.VMEM((8, HD), F32),
            pltpu.VMEM((HEADS, BLK, HD), BF16),
            pltpu.VMEM((HEADS, BLK, HD), BF16),
            pltpu.VMEM((HEADS, BLK, HD), BF16),
            pltpu.VMEM((HEADS, BLK, HD), BF16),
            DMA((4, HEADS)),
            DMA((SLOTS,)),
            DMA((SLOTS, 2)),
        ],
        compiler_params=pltpu.CompilerParams(vmem_limit_bytes=56 << 20),
        cost_estimate=pl.CostEstimate(flops=8 << 30, bytes_accessed=16 << 20, transcendentals=9 << 20),
        name="attention",
    )(seq_lengths, queries, d_out, *blocks)


def swap_core(value):
    return lax.ppermute(value, "core", [(0, 1), (1, 0)])


def swap_z(value, sources=(0, 1)):
    pairs = [(2 * zh + zl, 2 * (1 - zh) + (1 - zl)) for zh in sources for zl in range(2)]
    return lax.ppermute(value, ("zh", "zl"), pairs)


def swap_head(value):
    return lax.ppermute(value, "zl", [(0, 1), (1, 0)])


def shift_row(value, by):
    return lax.ppermute(value, ("x", "y"), [(r, (r + by) % 16) for r in range(16)])


def added(*values):
    total = values[0].astype(F32)
    for value in values[1:]:
        total = total + value.astype(F32)
    return total.astype(BF16)


def shift_both(value):
    same = shift_row(value, -1)
    pairs = [(2 * r + zl, 2 * ((r - 1) % 16) + 1 - zl) for r in range(16) for zl in range(2)]
    return same, lax.ppermute(value, ("x", "y", "zl"), pairs)


def returned(keep, send):
    first = lax.axis_index("zh") == 0
    zero = jnp.zeros((), BF16)
    given = [swap_core(part) for part in send]
    outer, middle = [], []
    for n, (a, b) in enumerate(zip(keep, given)):
        outer.append(added(jnp.where(first, a[2, 1], a[0, 1]), jnp.where(first, b[2, 1], b[0, 1])))
        a, b, outer[n] = lax.optimization_barrier((a, b, outer[n]))
        keep, given = [*keep[:n], a, *keep[n + 1:]], [*given[:n], b, *given[n + 1:]]
        middle.append(added(a[1, 1], b[1, 1]))
    outer = [swap_z(value) for value in outer]
    middle = [swap_z(lax.optimization_barrier(both)[0]) for both in zip(middle, outer)]
    back = [
        shift_row(added(a[2, 0], b[2, 0], jnp.where(first, zero, far)), -1) for a, b, far in zip(keep, given, outer)
    ]
    halves = [added(a[0, 0], b[0, 0], jnp.where(first, far, zero)) for a, b, far in zip(keep, given, outer)]
    others = [swap_head(half) for half in halves]
    done = []
    for a, b, near, far, half, other in zip(keep, given, middle, back, halves, others):
        same, cross = (value.astype(F32) for value in shift_both(added(a[1, 0], b[1, 0], near, far)))
        done.append(((half.astype(F32) + other.astype(F32)) + (same + cross)).astype(BF16))
    return done


def on_device(queries, key_rows, value_rows, d_out, seq_lengths):
    own = jnp.stack([key_rows, value_rows])
    row1 = shift_row(own, 1)
    side0 = swap_z(own, (0,))
    row2 = shift_row(row1, 1)
    side1 = swap_z(lax.optimization_barrier((row1, side0))[0])
    side2 = swap_z(row2, (1,))
    blocks = []
    for block in (own, side0, row1, side1, row2, side2):
        blocks += [block, swap_core(block)]
    attended, grad_queries, *parts = attention(seq_lengths, queries, d_out, blocks)
    grad_keys, grad_values = returned(parts[::2], parts[1::2])
    return attended, grad_queries, grad_keys, grad_values


def solution(mesh):
    fine = Mesh(mesh.devices.reshape(4, 4, 2, 2, 2), ("x", "y", "zh", "core", "zl"))
    tokens = P("zl", SEQ, None)
    rows = P(SEQ, None)
    return jax.shard_map(
        on_device,
        mesh=fine,
        in_specs=(tokens, rows, rows, tokens, P()),
        out_specs=(tokens, tokens, rows, rows),
        check_vma=False,
    )
```

```python
import math

import jax
import jax.numpy as jnp
from jax import lax
from jax.experimental import pallas as pl
from jax.experimental.pallas import tpu as pltpu
from jax.sharding import Mesh, PartitionSpec as P

NEGATIVE = -1e30
BLK = 512
HEADS = 4
HD = 128
NQ = HEADS * BLK
HALF = BLK // 2
ROWS = 3
SLOTS = 4 * ROWS
GROUP = 3
SPAN = 9
SCALE = HD ** -0.5
LOG2 = SCALE * math.log2(math.e)
BOUND = 64.0
F32 = jnp.float32
BF16 = jnp.bfloat16
SEQ = ("x", "y", "zh", "core")
VMEM = pl.BlockSpec(memory_space=pltpu.VMEM)
SMEM = pl.BlockSpec(memory_space=pltpu.SMEM)
ANY = pl.BlockSpec(memory_space=pl.ANY)
DMA = pltpu.SemaphoreType.DMA
NEAR = [(dz, dc) for dz in range(2) for dc in range(2)]


def shape(dims, dtype):
    return jax.ShapeDtypeStruct(dims, dtype)


def dot(a, b):
    return lax.dot_general(a, b, (((1,), (0,)), ((), ())), preferred_element_type=F32)


class Place:
    def __init__(self, len_ref):
        row = lax.axis_index("x") * 4 + lax.axis_index("y")
        self.zh = lax.axis_index("zh")
        self.core = lax.axis_index("core")
        place = self.zh * 2 + self.core
        base = (row - 2) * (4 * BLK)
        first = base + (8 + place) * BLK
        self.q_pos = lax.broadcasted_iota(jnp.int32, (1, BLK), 1) + (8 + place) * BLK
        starts = jnp.zeros((1, BLK), jnp.int32) - base
        first_start = -base
        last_start = -base
        end = jnp.int32(0)
        for c in range(16):
            end = end + len_ref[c]
            rel = end - base
            starts = jnp.where(self.q_pos >= rel, rel, starts)
            first_start = jnp.where(end <= first, rel, first_start)
            last_start = jnp.where(end <= first + BLK - 1, rel, last_start)
        self.starts = starts
        self.last_start = last_start
        self.lo = first_start // BLK
        self.hi = 8 + place

    def slot(self, j, dz, dc):
        return (2 - j) * 4 + (1 - self.zh if dz else self.zh) * 2 + (1 - self.core if dc else self.core)

    def mask(self, t):
        k_pos = lax.broadcasted_iota(jnp.int32, (BLK, BLK), 0) + t * BLK
        return (k_pos >= self.starts) & (k_pos <= self.q_pos)


def attention_kernel(*refs):
    len_ref, q_hbm, do_hbm = refs[:3]
    kv_refs = refs[3:15]
    o_hbm, dq_hbm = refs[15:17]
    out_refs = refs[17:21]
    kvs, dkvs, qt, dot_t, do_s, probs, row_max, total, acc, dq_acc, stage, delta, norms, q_ref, do_ref, o_ref, dq_ref, row_sem, in_sem, out_sem = refs[21:]
    loads = [[pltpu.make_async_copy(a.at[h], b.at[h], row_sem.at[n, h]) for n, (a, b) in enumerate(((q_hbm, q_ref), (do_hbm, do_ref)))] for h in range(HEADS)]
    for pair in loads:
        for copy in pair:
            copy.start()
    at = Place(len_ref)
    order = [(j, dz, dc) for j in range(ROWS) for dz, dc in NEAR]
    for n, where in enumerate(order):
        slot = at.slot(*where)
        pltpu.make_async_copy(kv_refs[n], kvs.at[slot], in_sem.at[slot]).start()

    def arrived(t):
        pltpu.make_async_copy(kv_refs[0], kvs.at[t], in_sem.at[t]).wait()

    def out_copy(n, part, t):
        j, dz, dc = order[n]
        return pltpu.make_async_copy(dkvs.at[t, part], out_refs[part * 2 + dc].at[j, dz], out_sem.at[n, part])

    begin = at.lo
    end = begin + (at.hi - begin + GROUP) // GROUP * GROUP
    for spare in range(SLOTS, SLOTS + GROUP - 1):
        kvs[spare] = jnp.zeros((2, BLK, HD), BF16)
    dkvs[SLOTS + GROUP - 1] = jnp.zeros((2, BLK, HD), BF16)
    for n, where in enumerate(order):
        slot = at.slot(*where)

        @pl.when((slot < begin) | (slot >= end))
        def _():
            for part in range(2):
                out_copy(n, part, SLOTS + GROUP - 1).start()

    for h in range(HEADS):
        cols = slice(h * BLK, (h + 1) * BLK)
        for copy in loads[h]:
            copy.wait()
        qt[:, cols] = q_ref[h].T
        dot_t[:, cols] = do_ref[h].T
    dq_acc[...] = jnp.zeros((HD, NQ), F32)
    norms[...] = jnp.zeros((8, HD), F32)

    def forward(t, masked, shift):
        k = kvs[t, 0]
        v_t = kvs[t, 1].T
        if not shift:
            squares = dot(jnp.square(k.astype(F32)).astype(BF16), jnp.ones((HD, HD), BF16))
            norms[...] = jnp.maximum(norms[...], jnp.max(squares.reshape(BLK // 8, 8, HD), axis=0))
        if masked:
            allowed = at.mask(t)

        def score(h):
            s = dot(k, qt[:, h * HALF:(h + 1) * HALF])
            return jnp.where(allowed[:, (h % 2) * HALF:(h % 2 + 1) * HALF], s, NEGATIVE) if masked else s

        def soft(h, s):
            cols = slice(h * HALF, (h + 1) * HALF)
            p = jnp.exp2(s * LOG2 - row_max[:, cols] if shift else s * LOG2)
            total[:, cols] += jnp.sum(p, axis=0, keepdims=True)
            p = p.astype(BF16)
            probs[t - begin, :, cols] = p
            return p

        def product(h, p):
            acc[:, h * HALF:(h + 1) * HALF] += dot(v_t, p)

        weights = soft(0, score(0))
        s = score(1)
        for h in range(1, 2 * HEADS):
            held, weights = weights, soft(h, s)
            if h + 1 < 2 * HEADS:
                s = score(h + 1)
            product(h - 1, held)
        product(2 * HEADS - 1, weights)

    def clear():
        total[...] = jnp.zeros((1, NQ), F32)
        acc[...] = jnp.zeros((HD, NQ), F32)

    def fast_step(i, carry):
        for u in range(GROUP):
            t = begin + i * GROUP + u

            @pl.when(t < SLOTS)
            def _():
                arrived(t)

        for u in range(GROUP):
            forward(begin + i * GROUP + u, True, False)

        return carry

    def max_step(t, carry):
        allowed = at.mask(t)
        for h in range(HEADS):
            cols = slice(h * BLK, (h + 1) * BLK)
            s = jnp.where(allowed, dot(kvs[t, 0], qt[:, cols]), NEGATIVE)
            row_max[:, cols] = jnp.maximum(row_max[:, cols], jnp.max(s, axis=0, keepdims=True))
        return carry

    def slow_step(t, carry):
        forward(t, True, True)
        return carry

    clear()
    lax.fori_loop(0, (end - begin) // GROUP, fast_step, 0)
    q_norm = jnp.max(dot(jnp.ones((8, HD), BF16), jnp.square(qt[...].astype(F32)).astype(BF16)))

    @pl.when(q_norm * jnp.max(norms[...]) > 0.98 * (BOUND / LOG2) ** 2)
    def _():
        clear()
        row_max[...] = jnp.full((1, NQ), NEGATIVE, F32)
        lax.fori_loop(begin, end, max_step, 0)
        row_max[...] = row_max[...] * LOG2
        lax.fori_loop(begin, end, slow_step, 0)

    for h in range(HEADS):
        cols = slice(h * BLK, (h + 1) * BLK)
        inverse = 1.0 / total[:, cols]
        o = (acc[:, cols] * inverse).astype(BF16)
        o_ref[h] = o.T
        pltpu.make_async_copy(o_ref.at[h], o_hbm.at[h], row_sem.at[2, h]).start()
        scaled = (dot_t[:, cols].astype(F32) * inverse).astype(BF16)
        dot_t[:, cols] = scaled
        do_s[h * BLK:(h + 1) * BLK] = scaled.T
        delta[:, cols] = jnp.sum(o.astype(F32) * scaled.astype(F32), axis=0, keepdims=True)

    def backward_tile(t, u):
        v = kvs[t, 1]

        def dp_of(h):
            return dot(v, dot_t[:, h * BLK:(h + 1) * BLK])

        def ds_of(h, dp):
            cols = slice(h * BLK, (h + 1) * BLK)
            ds = (probs[t - begin, :, cols].astype(F32) * (dp - delta[:, cols])).astype(BF16)
            stage[u * BLK:(u + 1) * BLK, cols] = ds
            return ds

        d0 = dp_of(0)
        d1 = dp_of(1)
        ds_of(0, d0)
        dkvs[t, 1] = dot(probs[t - begin], do_s[...]).astype(BF16)
        d2 = dp_of(2)
        ds_of(1, d1)
        d3 = dp_of(3)
        ds_of(2, d2)
        ds_of(3, d3)
        dkvs[t, 0] = (dot(stage[u * BLK:(u + 1) * BLK], q_ref[...].reshape(NQ, HD)) * SCALE).astype(BF16)

    def backward_step(i, carry):
        first = begin + i * GROUP
        for u in range(GROUP):
            backward_tile(first + u, u)
        k_t = jnp.concatenate([kvs[first + u, 0].T for u in range(GROUP)], axis=1)
        for h in range(HEADS):
            cols = slice(h * BLK, (h + 1) * BLK)
            dq_acc[:, cols] += dot(k_t, stage[:, cols])
        for n, where in enumerate(order):
            slot = at.slot(*where)

            @pl.when((slot >= first) & (slot < first + GROUP))
            def _():
                for part in range(2):
                    out_copy(n, part, slot).start()

        return carry

    lax.fori_loop(0, (end - begin) // GROUP, backward_step, 0)
    for h in range(HEADS):
        dq_ref[h] = (dq_acc[:, h * BLK:(h + 1) * BLK] * SCALE).astype(BF16).T
        pltpu.make_async_copy(dq_ref.at[h], dq_hbm.at[h], row_sem.at[3, h]).start()

    def rest(t, carry):
        arrived(t)
        return carry

    lax.fori_loop(0, begin, rest, 0)
    lax.fori_loop(jnp.minimum(end, SLOTS), SLOTS, rest, 0)
    for n in range(len(order)):
        for part in range(2):
            out_copy(n, part, 0).wait()
    for h in range(HEADS):
        pltpu.make_async_copy(o_ref.at[h], o_hbm.at[h], row_sem.at[2, h]).wait()
        pltpu.make_async_copy(dq_ref.at[h], dq_hbm.at[h], row_sem.at[3, h]).wait()


def attention(seq_lengths, queries, d_out, blocks):
    rows = shape((HEADS, BLK, HD), BF16)
    grads = shape((ROWS, 2, BLK, HD), BF16)
    return pl.pallas_call(
        attention_kernel,
        out_shape=(rows, rows) + (grads,) * 4,
        in_specs=[SMEM] + [ANY] * (2 + SLOTS),
        out_specs=[ANY] * 6,
        scratch_shapes=[
            pltpu.VMEM((SLOTS + GROUP - 1, 2, BLK, HD), BF16),
            pltpu.VMEM((SLOTS + GROUP, 2, BLK, HD), BF16),
            pltpu.VMEM((HD, NQ), BF16),
            pltpu.VMEM((HD, NQ), BF16),
            pltpu.VMEM((NQ, HD), BF16),
            pltpu.VMEM((SPAN, BLK, NQ), BF16),
            pltpu.VMEM((1, NQ), F32),
            pltpu.VMEM((1, NQ), F32),
            pltpu.VMEM((HD, NQ), F32),
            pltpu.VMEM((HD, NQ), F32),
            pltpu.VMEM((GROUP * BLK, NQ), BF16),
            pltpu.VMEM((1, NQ), F32),
            pltpu.VMEM((8, HD), F32),
            pltpu.VMEM((HEADS, BLK, HD), BF16),
            pltpu.VMEM((HEADS, BLK, HD), BF16),
            pltpu.VMEM((HEADS, BLK, HD), BF16),
            pltpu.VMEM((HEADS, BLK, HD), BF16),
            DMA((4, HEADS)),
            DMA((SLOTS,)),
            DMA((SLOTS, 2)),
        ],
        compiler_params=pltpu.CompilerParams(vmem_limit_bytes=56 << 20),
        cost_estimate=pl.CostEstimate(flops=8 << 30, bytes_accessed=16 << 20, transcendentals=9 << 20),
        name="attention",
    )(seq_lengths, queries, d_out, *blocks)


def swap_core(value):
    return lax.ppermute(value, "core", [(0, 1), (1, 0)])


def swap_z(value, sources=(0, 1)):
    pairs = [(2 * zh + zl, 2 * (1 - zh) + (1 - zl)) for zh in sources for zl in range(2)]
    return lax.ppermute(value, ("zh", "zl"), pairs)


def swap_head(value):
    return lax.ppermute(value, "zl", [(0, 1), (1, 0)])


def shift_row(value, by):
    return lax.ppermute(value, ("x", "y"), [(r, (r + by) % 16) for r in range(16)])


def added(*values):
    total = values[0].astype(F32)
    for value in values[1:]:
        total = total + value.astype(F32)
    return total.astype(BF16)


def shift_both(value):
    same = shift_row(value, -1)
    pairs = [(2 * r + zl, 2 * ((r - 1) % 16) + 1 - zl) for r in range(16) for zl in range(2)]
    return same, lax.ppermute(value, ("x", "y", "zl"), pairs)


def returned(keep, send):
    first = lax.axis_index("zh") == 0
    zero = jnp.zeros((), BF16)
    given = [swap_core(part) for part in send]
    outer, middle = [], []
    for a, b in zip(keep, given):
        outer.append(added(jnp.where(first, a[2, 1], a[0, 1]), jnp.where(first, b[2, 1], b[0, 1])))
        middle.append(added(a[1, 1], b[1, 1]))
    outer = [swap_z(value) for value in outer]
    middle = [swap_z(lax.optimization_barrier(both)[0]) for both in zip(middle, outer)]
    back = [
        shift_row(added(a[2, 0], b[2, 0], jnp.where(first, zero, far)), -1) for a, b, far in zip(keep, given, outer)
    ]
    halves = [added(a[0, 0], b[0, 0], jnp.where(first, far, zero)) for a, b, far in zip(keep, given, outer)]
    done = []
    for a, b, near, far, half in zip(keep, given, middle, back, halves):
        both, half = lax.optimization_barrier((added(a[1, 0], b[1, 0], near, far), half))
        same, cross = (value.astype(F32) for value in shift_both(both))
        done.append(((half.astype(F32) + swap_head(half).astype(F32)) + (same + cross)).astype(BF16))
    return done


def on_device(queries, key_rows, value_rows, d_out, seq_lengths):
    own = jnp.stack([key_rows, value_rows])
    row1 = shift_row(own, 1)
    side0 = swap_z(own, (0,))
    row2 = shift_row(row1, 1)
    side1 = swap_z(lax.optimization_barrier((row1, side0))[0])
    side2 = swap_z(row2, (1,))
    blocks = []
    for block in (own, side0, row1, side1, row2, side2):
        blocks += [block, swap_core(block)]
    attended, grad_queries, *parts = attention(seq_lengths, queries, d_out, blocks)
    grad_keys, grad_values = returned(parts[::2], parts[1::2])
    return attended, grad_queries, grad_keys, grad_values


def solution(mesh):
    fine = Mesh(mesh.devices.reshape(4, 4, 2, 2, 2), ("x", "y", "zh", "core", "zl"))
    tokens = P("zl", SEQ, None)
    rows = P(SEQ, None)
    return jax.shard_map(
        on_device,
        mesh=fine,
        in_specs=(tokens, rows, rows, tokens, P()),
        out_specs=(tokens, tokens, rows, rows),
        check_vma=False,
    )
```

```python
import math

import jax
import jax.numpy as jnp
from jax import lax
from jax.experimental import pallas as pl
from jax.experimental.pallas import tpu as pltpu
from jax.sharding import Mesh, PartitionSpec as P

NEGATIVE = -1e30
BLK = 512
HEADS = 4
HD = 128
NQ = HEADS * BLK
HALF = BLK // 2
ROWS = 3
SLOTS = 4 * ROWS
GROUP = 3
SPAN = 9
SCALE = HD ** -0.5
LOG2 = SCALE * math.log2(math.e)
BOUND = 64.0
F32 = jnp.float32
BF16 = jnp.bfloat16
SEQ = ("x", "y", "zh", "core")
VMEM = pl.BlockSpec(memory_space=pltpu.VMEM)
SMEM = pl.BlockSpec(memory_space=pltpu.SMEM)
ANY = pl.BlockSpec(memory_space=pl.ANY)
DMA = pltpu.SemaphoreType.DMA
NEAR = [(dz, dc) for dz in range(2) for dc in range(2)]


def shape(dims, dtype):
    return jax.ShapeDtypeStruct(dims, dtype)


def dot(a, b):
    return lax.dot_general(a, b, (((1,), (0,)), ((), ())), preferred_element_type=F32)


class Place:
    def __init__(self, len_ref):
        row = lax.axis_index("x") * 4 + lax.axis_index("y")
        self.zh = lax.axis_index("zh")
        self.core = lax.axis_index("core")
        place = self.zh * 2 + self.core
        base = (row - 2) * (4 * BLK)
        first = base + (8 + place) * BLK
        self.q_pos = lax.broadcasted_iota(jnp.int32, (1, BLK), 1) + (8 + place) * BLK
        starts = jnp.zeros((1, BLK), jnp.int32) - base
        first_start = -base
        last_start = -base
        end = jnp.int32(0)
        for c in range(16):
            end = end + len_ref[c]
            rel = end - base
            starts = jnp.where(self.q_pos >= rel, rel, starts)
            first_start = jnp.where(end <= first, rel, first_start)
            last_start = jnp.where(end <= first + BLK - 1, rel, last_start)
        self.starts = starts
        self.last_start = last_start
        self.lo = first_start // BLK
        self.hi = 8 + place

    def slot(self, j, dz, dc):
        return (2 - j) * 4 + (1 - self.zh if dz else self.zh) * 2 + (1 - self.core if dc else self.core)

    def mask(self, t):
        k_pos = lax.broadcasted_iota(jnp.int32, (BLK, BLK), 0) + t * BLK
        return (k_pos >= self.starts) & (k_pos <= self.q_pos)


def attention_kernel(*refs):
    len_ref, q_hbm, do_hbm = refs[:3]
    kv_refs = refs[3:15]
    o_hbm, dq_hbm = refs[15:17]
    out_refs = refs[17:19]
    kvs, dkvs, qt, dot_t, do_s, probs, row_max, total, acc, dq_acc, stage, delta, norms, q_ref, do_ref, o_ref, dq_ref, row_sem, in_sem, out_sem = refs[19:]
    loads = [[pltpu.make_async_copy(a.at[h], b.at[h], row_sem.at[n, h]) for n, (a, b) in enumerate(((q_hbm, q_ref), (do_hbm, do_ref)))] for h in range(HEADS)]
    for pair in loads:
        for copy in pair:
            copy.start()
    at = Place(len_ref)
    order = [(j, dz, dc) for j in range(ROWS) for dz, dc in NEAR]
    for n, where in enumerate(order):
        slot = at.slot(*where)
        pltpu.make_async_copy(kv_refs[n], kvs.at[slot], in_sem.at[slot]).start()

    def arrived(t):
        pltpu.make_async_copy(kv_refs[0], kvs.at[t], in_sem.at[t]).wait()

    def out_copy(n, t):
        j, dz, dc = order[n]
        return pltpu.make_async_copy(dkvs.at[t], out_refs[dc].at[j, dz], out_sem.at[n])

    begin = at.lo
    end = begin + (at.hi - begin + GROUP) // GROUP * GROUP
    for spare in range(SLOTS, SLOTS + GROUP - 1):
        kvs[spare] = jnp.zeros((2, BLK, HD), BF16)
    dkvs[SLOTS + GROUP - 1] = jnp.zeros((2, BLK, HD), BF16)
    for n, where in enumerate(order):
        slot = at.slot(*where)

        @pl.when((slot < begin) | (slot >= end))
        def _():
            out_copy(n, SLOTS + GROUP - 1).start()

    for h in range(HEADS):
        cols = slice(h * BLK, (h + 1) * BLK)
        for copy in loads[h]:
            copy.wait()
        qt[:, cols] = q_ref[h].T
        dot_t[:, cols] = do_ref[h].T
    dq_acc[...] = jnp.zeros((HD, NQ), F32)
    norms[...] = jnp.zeros((8, HD), F32)

    def forward(t, masked, shift):
        k = kvs[t, 0]
        v_t = kvs[t, 1].T
        if not shift:
            squares = dot(jnp.square(k.astype(F32)).astype(BF16), jnp.ones((HD, HD), BF16))
            norms[...] = jnp.maximum(norms[...], jnp.max(squares.reshape(BLK // 8, 8, HD), axis=0))
        if masked:
            allowed = at.mask(t)

        def score(h):
            s = dot(k, qt[:, h * HALF:(h + 1) * HALF])
            return jnp.where(allowed[:, (h % 2) * HALF:(h % 2 + 1) * HALF], s, NEGATIVE) if masked else s

        def soft(h, s):
            cols = slice(h * HALF, (h + 1) * HALF)
            p = jnp.exp2(s * LOG2 - row_max[:, cols] if shift else s * LOG2)
            total[:, cols] += jnp.sum(p, axis=0, keepdims=True)
            p = p.astype(BF16)
            probs[t - begin, :, cols] = p
            return p

        def product(h, p):
            acc[:, h * HALF:(h + 1) * HALF] += dot(v_t, p)

        weights = soft(0, score(0))
        s = score(1)
        for h in range(1, 2 * HEADS):
            held, weights = weights, soft(h, s)
            if h + 1 < 2 * HEADS:
                s = score(h + 1)
            product(h - 1, held)
        product(2 * HEADS - 1, weights)

    def clear():
        total[...] = jnp.zeros((1, NQ), F32)
        acc[...] = jnp.zeros((HD, NQ), F32)

    def fast_step(i, carry):
        for u in range(GROUP):
            t = begin + i * GROUP + u

            @pl.when(t < SLOTS)
            def _():
                arrived(t)

        for u in range(GROUP):
            forward(begin + i * GROUP + u, True, False)

        return carry

    def max_step(t, carry):
        allowed = at.mask(t)
        for h in range(HEADS):
            cols = slice(h * BLK, (h + 1) * BLK)
            s = jnp.where(allowed, dot(kvs[t, 0], qt[:, cols]), NEGATIVE)
            row_max[:, cols] = jnp.maximum(row_max[:, cols], jnp.max(s, axis=0, keepdims=True))
        return carry

    def slow_step(t, carry):
        forward(t, True, True)
        return carry

    clear()
    lax.fori_loop(0, (end - begin) // GROUP, fast_step, 0)
    q_norm = jnp.max(dot(jnp.ones((8, HD), BF16), jnp.square(qt[...].astype(F32)).astype(BF16)))

    @pl.when(q_norm * jnp.max(norms[...]) > 0.98 * (BOUND / LOG2) ** 2)
    def _():
        clear()
        row_max[...] = jnp.full((1, NQ), NEGATIVE, F32)
        lax.fori_loop(begin, end, max_step, 0)
        row_max[...] = row_max[...] * LOG2
        lax.fori_loop(begin, end, slow_step, 0)

    for h in range(HEADS):
        cols = slice(h * BLK, (h + 1) * BLK)
        inverse = 1.0 / total[:, cols]
        o = (acc[:, cols] * inverse).astype(BF16)
        o_ref[h] = o.T
        pltpu.make_async_copy(o_ref.at[h], o_hbm.at[h], row_sem.at[2, h]).start()
        scaled = (dot_t[:, cols].astype(F32) * inverse).astype(BF16)
        dot_t[:, cols] = scaled
        do_s[h * BLK:(h + 1) * BLK] = scaled.T
        delta[:, cols] = jnp.sum(o.astype(F32) * scaled.astype(F32), axis=0, keepdims=True)

    def backward_tile(t, u):
        v = kvs[t, 1]

        def dp_of(h):
            return dot(v, dot_t[:, h * BLK:(h + 1) * BLK])

        def ds_of(h, dp):
            cols = slice(h * BLK, (h + 1) * BLK)
            ds = (probs[t - begin, :, cols].astype(F32) * (dp - delta[:, cols])).astype(BF16)
            stage[u * BLK:(u + 1) * BLK, cols] = ds
            return ds

        d0 = dp_of(0)
        d1 = dp_of(1)
        ds_of(0, d0)
        dkvs[t, 1] = dot(probs[t - begin], do_s[...]).astype(BF16)
        d2 = dp_of(2)
        ds_of(1, d1)
        d3 = dp_of(3)
        ds_of(2, d2)
        ds_of(3, d3)
        dkvs[t, 0] = (dot(stage[u * BLK:(u + 1) * BLK], q_ref[...].reshape(NQ, HD)) * SCALE).astype(BF16)

    def backward_step(i, carry):
        first = begin + i * GROUP
        for u in range(GROUP):
            backward_tile(first + u, u)
        k_t = jnp.concatenate([kvs[first + u, 0].T for u in range(GROUP)], axis=1)
        for h in range(HEADS):
            cols = slice(h * BLK, (h + 1) * BLK)
            dq_acc[:, cols] += dot(k_t, stage[:, cols])
        for n, where in enumerate(order):
            slot = at.slot(*where)

            @pl.when((slot >= first) & (slot < first + GROUP))
            def _():
                out_copy(n, slot).start()

        return carry

    lax.fori_loop(0, (end - begin) // GROUP, backward_step, 0)
    for h in range(HEADS):
        dq_ref[h] = (dq_acc[:, h * BLK:(h + 1) * BLK] * SCALE).astype(BF16).T
        pltpu.make_async_copy(dq_ref.at[h], dq_hbm.at[h], row_sem.at[3, h]).start()

    def rest(t, carry):
        arrived(t)
        return carry

    lax.fori_loop(0, begin, rest, 0)
    lax.fori_loop(jnp.minimum(end, SLOTS), SLOTS, rest, 0)
    for n in range(len(order)):
        out_copy(n, 0).wait()
    for h in range(HEADS):
        pltpu.make_async_copy(o_ref.at[h], o_hbm.at[h], row_sem.at[2, h]).wait()
        pltpu.make_async_copy(dq_ref.at[h], dq_hbm.at[h], row_sem.at[3, h]).wait()


def attention(seq_lengths, queries, d_out, blocks):
    rows = shape((HEADS, BLK, HD), BF16)
    grads = shape((ROWS, 2, 2, BLK, HD), BF16)
    return pl.pallas_call(
        attention_kernel,
        out_shape=(rows, rows) + (grads,) * 2,
        in_specs=[SMEM] + [ANY] * (2 + SLOTS),
        out_specs=[ANY] * 4,
        scratch_shapes=[
            pltpu.VMEM((SLOTS + GROUP - 1, 2, BLK, HD), BF16),
            pltpu.VMEM((SLOTS + GROUP, 2, BLK, HD), BF16),
            pltpu.VMEM((HD, NQ), BF16),
            pltpu.VMEM((HD, NQ), BF16),
            pltpu.VMEM((NQ, HD), BF16),
            pltpu.VMEM((SPAN, BLK, NQ), BF16),
            pltpu.VMEM((1, NQ), F32),
            pltpu.VMEM((1, NQ), F32),
            pltpu.VMEM((HD, NQ), F32),
            pltpu.VMEM((HD, NQ), F32),
            pltpu.VMEM((GROUP * BLK, NQ), BF16),
            pltpu.VMEM((1, NQ), F32),
            pltpu.VMEM((8, HD), F32),
            pltpu.VMEM((HEADS, BLK, HD), BF16),
            pltpu.VMEM((HEADS, BLK, HD), BF16),
            pltpu.VMEM((HEADS, BLK, HD), BF16),
            pltpu.VMEM((HEADS, BLK, HD), BF16),
            DMA((4, HEADS)),
            DMA((SLOTS,)),
            DMA((SLOTS,)),
        ],
        compiler_params=pltpu.CompilerParams(vmem_limit_bytes=56 << 20),
        cost_estimate=pl.CostEstimate(flops=8 << 30, bytes_accessed=16 << 20, transcendentals=9 << 20),
        name="attention",
    )(seq_lengths, queries, d_out, *blocks)


def swap_core(value):
    return lax.ppermute(value, "core", [(0, 1), (1, 0)])


def swap_z(value, sources=(0, 1)):
    pairs = [(2 * zh + zl, 2 * (1 - zh) + (1 - zl)) for zh in sources for zl in range(2)]
    return lax.ppermute(value, ("zh", "zl"), pairs)


def swap_head(value):
    return lax.ppermute(value, "zl", [(0, 1), (1, 0)])


def shift_row(value, by):
    return lax.ppermute(value, ("x", "y"), [(r, (r + by) % 16) for r in range(16)])


def added(*values):
    total = values[0].astype(F32)
    for value in values[1:]:
        total = total + value.astype(F32)
    return total.astype(BF16)


def returned(keep, send):
    first = lax.axis_index("zh") == 0
    zero = jnp.zeros((), BF16)
    given = swap_core(send)
    outer = swap_z(added(jnp.where(first, keep[2, 1], keep[0, 1]), jnp.where(first, given[2, 1], given[0, 1])))
    middle = added(keep[1, 1], given[1, 1])
    middle, outer = lax.optimization_barrier((middle, outer))
    middle = swap_z(middle)
    back = shift_row(added(keep[2, 0], given[2, 0], jnp.where(first, zero, outer)), -1)
    back = shift_row(added(keep[1, 0], given[1, 0], middle, back), -1)
    half = added(keep[0, 0], given[0, 0], jnp.where(first, outer, zero), back)
    other = swap_head(half)
    return [added(half[part], other[part]) for part in range(2)]


def on_device(queries, key_rows, value_rows, d_out, seq_lengths):
    own = jnp.stack([key_rows, value_rows])
    row1 = shift_row(own, 1)
    side0 = swap_z(own, (0,))
    row2 = shift_row(row1, 1)
    side1 = swap_z(lax.optimization_barrier((row1, side0))[0])
    side2 = swap_z(row2, (1,))
    blocks = []
    for block in (own, side0, row1, side1, row2, side2):
        blocks += [block, swap_core(block)]
    attended, grad_queries, *parts = attention(seq_lengths, queries, d_out, blocks)
    grad_keys, grad_values = returned(*parts)
    return attended, grad_queries, grad_keys, grad_values


def solution(mesh):
    fine = Mesh(mesh.devices.reshape(4, 4, 2, 2, 2), ("x", "y", "zh", "core", "zl"))
    tokens = P("zl", SEQ, None)
    rows = P(SEQ, None)
    return jax.shard_map(
        on_device,
        mesh=fine,
        in_specs=(tokens, rows, rows, tokens, P()),
        out_specs=(tokens, tokens, rows, rows),
        check_vma=False,
    )
```

```python
import math

import jax
import jax.numpy as jnp
from jax import lax
from jax.experimental import pallas as pl
from jax.experimental.pallas import tpu as pltpu
from jax.sharding import Mesh, PartitionSpec as P

NEGATIVE = -1e30
BLK = 512
HEADS = 4
HD = 128
NQ = HEADS * BLK
HALF = BLK // 2
ROWS = 3
SLOTS = 4 * ROWS
GROUP = 3
SPAN = 9
SCALE = HD ** -0.5
LOG2 = SCALE * math.log2(math.e)
BOUND = 64.0
F32 = jnp.float32
BF16 = jnp.bfloat16
SEQ = ("x", "y", "zh", "core")
VMEM = pl.BlockSpec(memory_space=pltpu.VMEM)
SMEM = pl.BlockSpec(memory_space=pltpu.SMEM)
ANY = pl.BlockSpec(memory_space=pl.ANY)
DMA = pltpu.SemaphoreType.DMA
NEAR = [(dz, dc) for dz in range(2) for dc in range(2)]


def shape(dims, dtype):
    return jax.ShapeDtypeStruct(dims, dtype)


def dot(a, b):
    return lax.dot_general(a, b, (((1,), (0,)), ((), ())), preferred_element_type=F32)


class Place:
    def __init__(self, len_ref):
        row = lax.axis_index("x") * 4 + lax.axis_index("y")
        self.zh = lax.axis_index("zh")
        self.core = lax.axis_index("core")
        place = self.zh * 2 + self.core
        base = (row - 2) * (4 * BLK)
        first = base + (8 + place) * BLK
        self.q_pos = lax.broadcasted_iota(jnp.int32, (1, BLK), 1) + (8 + place) * BLK
        starts = jnp.zeros((1, BLK), jnp.int32) - base
        first_start = -base
        last_start = -base
        end = jnp.int32(0)
        for c in range(16):
            end = end + len_ref[c]
            rel = end - base
            starts = jnp.where(self.q_pos >= rel, rel, starts)
            first_start = jnp.where(end <= first, rel, first_start)
            last_start = jnp.where(end <= first + BLK - 1, rel, last_start)
        self.starts = starts
        self.last_start = last_start
        self.lo = first_start // BLK
        self.hi = 8 + place

    def slot(self, j, dz, dc):
        return (2 - j) * 4 + (1 - self.zh if dz else self.zh) * 2 + (1 - self.core if dc else self.core)

    def mask(self, t):
        k_pos = lax.broadcasted_iota(jnp.int32, (BLK, BLK), 0) + t * BLK
        return (k_pos >= self.starts) & (k_pos <= self.q_pos)


def attention_kernel(*refs):
    len_ref, q_hbm, do_hbm = refs[:3]
    kv_refs = refs[3:17]
    o_hbm, dq_hbm = refs[17:19]
    out_refs = refs[19:23]
    kvs, dkvs, qt, dot_t, do_s, probs, row_max, total, acc, dq_acc, stage, delta, norms, q_ref, do_ref, o_ref, dq_ref, row_sem, in_sem, out_sem = refs[23:]
    loads = [[pltpu.make_async_copy(a.at[h], b.at[h], row_sem.at[n, h]) for n, (a, b) in enumerate(((q_hbm, q_ref), (do_hbm, do_ref)))] for h in range(HEADS)]
    for pair in loads:
        for copy in pair:
            copy.start()
    at = Place(len_ref)
    order = [(j, dz, dc) for j in range(ROWS) for dz, dc in NEAR]
    for n, where in enumerate(order):
        slot = at.slot(*where)
        if n < SLOTS - 2:
            pltpu.make_async_copy(kv_refs[n], kvs.at[slot], in_sem.at[slot]).start()
        else:
            for part in range(2):
                pltpu.make_async_copy(kv_refs[n + 2 * part], kvs.at[slot, part], in_sem.at[slot]).start()

    def arrived(t):
        pltpu.make_async_copy(kv_refs[0], kvs.at[t], in_sem.at[t]).wait()

    def out_copy(n, part, t):
        j, dz, dc = order[n]
        return pltpu.make_async_copy(dkvs.at[t, part], out_refs[part * 2 + dc].at[j, dz], out_sem.at[n, part])

    begin = at.lo
    end = begin + (at.hi - begin + GROUP) // GROUP * GROUP
    for spare in range(SLOTS, SLOTS + GROUP - 1):
        kvs[spare] = jnp.zeros((2, BLK, HD), BF16)
    dkvs[SLOTS + GROUP - 1] = jnp.zeros((2, BLK, HD), BF16)
    for n, where in enumerate(order):
        slot = at.slot(*where)

        @pl.when((slot < begin) | (slot >= end))
        def _():
            for part in range(2):
                out_copy(n, part, SLOTS + GROUP - 1).start()

    for h in range(HEADS):
        cols = slice(h * BLK, (h + 1) * BLK)
        for copy in loads[h]:
            copy.wait()
        qt[:, cols] = q_ref[h].T
        dot_t[:, cols] = do_ref[h].T
    dq_acc[...] = jnp.zeros((HD, NQ), F32)
    norms[...] = jnp.zeros((8, HD), F32)

    def forward(t, masked, shift):
        k = kvs[t, 0]
        v_t = kvs[t, 1].T
        if not shift:
            squares = dot(jnp.square(k.astype(F32)).astype(BF16), jnp.ones((HD, HD), BF16))
            norms[...] = jnp.maximum(norms[...], jnp.max(squares.reshape(BLK // 8, 8, HD), axis=0))
        if masked:
            allowed = at.mask(t)

        def score(h):
            s = dot(k, qt[:, h * HALF:(h + 1) * HALF])
            return jnp.where(allowed[:, (h % 2) * HALF:(h % 2 + 1) * HALF], s, NEGATIVE) if masked else s

        def soft(h, s):
            cols = slice(h * HALF, (h + 1) * HALF)
            p = jnp.exp2(s * LOG2 - row_max[:, cols] if shift else s * LOG2)
            total[:, cols] += jnp.sum(p, axis=0, keepdims=True)
            p = p.astype(BF16)
            probs[t - begin, :, cols] = p
            return p

        def product(h, p):
            acc[:, h * HALF:(h + 1) * HALF] += dot(v_t, p)

        weights = soft(0, score(0))
        s = score(1)
        for h in range(1, 2 * HEADS):
            held, weights = weights, soft(h, s)
            if h + 1 < 2 * HEADS:
                s = score(h + 1)
            product(h - 1, held)
        product(2 * HEADS - 1, weights)

    def clear():
        total[...] = jnp.zeros((1, NQ), F32)
        acc[...] = jnp.zeros((HD, NQ), F32)

    def fast_step(i, carry):
        for u in range(GROUP):
            t = begin + i * GROUP + u

            @pl.when(t < SLOTS)
            def _():
                arrived(t)

        for u in range(GROUP):
            forward(begin + i * GROUP + u, True, False)

        return carry

    def max_step(t, carry):
        allowed = at.mask(t)
        for h in range(HEADS):
            cols = slice(h * BLK, (h + 1) * BLK)
            s = jnp.where(allowed, dot(kvs[t, 0], qt[:, cols]), NEGATIVE)
            row_max[:, cols] = jnp.maximum(row_max[:, cols], jnp.max(s, axis=0, keepdims=True))
        return carry

    def slow_step(t, carry):
        forward(t, True, True)
        return carry

    clear()
    lax.fori_loop(0, (end - begin) // GROUP, fast_step, 0)
    q_norm = jnp.max(dot(jnp.ones((8, HD), BF16), jnp.square(qt[...].astype(F32)).astype(BF16)))

    @pl.when(q_norm * jnp.max(norms[...]) > 0.98 * (BOUND / LOG2) ** 2)
    def _():
        clear()
        row_max[...] = jnp.full((1, NQ), NEGATIVE, F32)
        lax.fori_loop(begin, end, max_step, 0)
        row_max[...] = row_max[...] * LOG2
        lax.fori_loop(begin, end, slow_step, 0)

    for h in range(HEADS):
        cols = slice(h * BLK, (h + 1) * BLK)
        inverse = 1.0 / total[:, cols]
        o = (acc[:, cols] * inverse).astype(BF16)
        o_ref[h] = o.T
        pltpu.make_async_copy(o_ref.at[h], o_hbm.at[h], row_sem.at[2, h]).start()
        scaled = (dot_t[:, cols].astype(F32) * inverse).astype(BF16)
        dot_t[:, cols] = scaled
        do_s[h * BLK:(h + 1) * BLK] = scaled.T
        delta[:, cols] = jnp.sum(o.astype(F32) * scaled.astype(F32), axis=0, keepdims=True)

    def backward_tile(t, u):
        v = kvs[t, 1]

        def dp_of(h):
            return dot(v, dot_t[:, h * BLK:(h + 1) * BLK])

        def ds_of(h, dp):
            cols = slice(h * BLK, (h + 1) * BLK)
            ds = (probs[t - begin, :, cols].astype(F32) * (dp - delta[:, cols])).astype(BF16)
            stage[u * BLK:(u + 1) * BLK, cols] = ds
            return ds

        d0 = dp_of(0)
        d1 = dp_of(1)
        ds_of(0, d0)
        dkvs[t, 1] = dot(probs[t - begin], do_s[...]).astype(BF16)
        d2 = dp_of(2)
        ds_of(1, d1)
        d3 = dp_of(3)
        ds_of(2, d2)
        ds_of(3, d3)
        dkvs[t, 0] = (dot(stage[u * BLK:(u + 1) * BLK], q_ref[...].reshape(NQ, HD)) * SCALE).astype(BF16)

    def backward_step(i, carry):
        first = begin + i * GROUP
        for u in range(GROUP):
            backward_tile(first + u, u)
        k_t = jnp.concatenate([kvs[first + u, 0].T for u in range(GROUP)], axis=1)
        for h in range(HEADS):
            cols = slice(h * BLK, (h + 1) * BLK)
            dq_acc[:, cols] += dot(k_t, stage[:, cols])
        for n, where in enumerate(order):
            slot = at.slot(*where)

            @pl.when((slot >= first) & (slot < first + GROUP))
            def _():
                for part in range(2):
                    out_copy(n, part, slot).start()

        return carry

    lax.fori_loop(0, (end - begin) // GROUP, backward_step, 0)
    for h in range(HEADS):
        dq_ref[h] = (dq_acc[:, h * BLK:(h + 1) * BLK] * SCALE).astype(BF16).T
        pltpu.make_async_copy(dq_ref.at[h], dq_hbm.at[h], row_sem.at[3, h]).start()

    def rest(t, carry):
        arrived(t)
        return carry

    lax.fori_loop(0, begin, rest, 0)
    lax.fori_loop(jnp.minimum(end, SLOTS), SLOTS, rest, 0)
    for n in range(len(order)):
        for part in range(2):
            out_copy(n, part, 0).wait()
    for h in range(HEADS):
        pltpu.make_async_copy(o_ref.at[h], o_hbm.at[h], row_sem.at[2, h]).wait()
        pltpu.make_async_copy(dq_ref.at[h], dq_hbm.at[h], row_sem.at[3, h]).wait()


def attention(seq_lengths, queries, d_out, blocks):
    rows = shape((HEADS, BLK, HD), BF16)
    grads = shape((ROWS, 2, BLK, HD), BF16)
    return pl.pallas_call(
        attention_kernel,
        out_shape=(rows, rows) + (grads,) * 4,
        in_specs=[SMEM] + [ANY] * (4 + SLOTS),
        out_specs=[ANY] * 6,
        scratch_shapes=[
            pltpu.VMEM((SLOTS + GROUP - 1, 2, BLK, HD), BF16),
            pltpu.VMEM((SLOTS + GROUP, 2, BLK, HD), BF16),
            pltpu.VMEM((HD, NQ), BF16),
            pltpu.VMEM((HD, NQ), BF16),
            pltpu.VMEM((NQ, HD), BF16),
            pltpu.VMEM((SPAN, BLK, NQ), BF16),
            pltpu.VMEM((1, NQ), F32),
            pltpu.VMEM((1, NQ), F32),
            pltpu.VMEM((HD, NQ), F32),
            pltpu.VMEM((HD, NQ), F32),
            pltpu.VMEM((GROUP * BLK, NQ), BF16),
            pltpu.VMEM((1, NQ), F32),
            pltpu.VMEM((8, HD), F32),
            pltpu.VMEM((HEADS, BLK, HD), BF16),
            pltpu.VMEM((HEADS, BLK, HD), BF16),
            pltpu.VMEM((HEADS, BLK, HD), BF16),
            pltpu.VMEM((HEADS, BLK, HD), BF16),
            DMA((4, HEADS)),
            DMA((SLOTS,)),
            DMA((SLOTS, 2)),
        ],
        compiler_params=pltpu.CompilerParams(vmem_limit_bytes=56 << 20),
        cost_estimate=pl.CostEstimate(flops=8 << 30, bytes_accessed=16 << 20, transcendentals=9 << 20),
        name="attention",
    )(seq_lengths, queries, d_out, *blocks)


def swap_core(value):
    return lax.ppermute(value, "core", [(0, 1), (1, 0)])


def swap_z(value, sources=(0, 1)):
    pairs = [(2 * zh + zl, 2 * (1 - zh) + (1 - zl)) for zh in sources for zl in range(2)]
    return lax.ppermute(value, ("zh", "zl"), pairs)


def swap_head(value):
    return lax.ppermute(value, "zl", [(0, 1), (1, 0)])


def shift_row(value, by):
    return lax.ppermute(value, ("x", "y"), [(r, (r + by) % 16) for r in range(16)])


def added(*values):
    total = values[0].astype(F32)
    for value in values[1:]:
        total = total + value.astype(F32)
    return total.astype(BF16)


def returned(keep, send):
    first = lax.axis_index("zh") == 0
    zero = jnp.zeros((), BF16)
    given = [swap_core(part) for part in send]
    outer, middle = [], []
    for a, b in zip(keep, given):
        outer.append(added(jnp.where(first, a[2, 1], a[0, 1]), jnp.where(first, b[2, 1], b[0, 1])))
        middle.append(added(a[1, 1], b[1, 1]))
    outer = [swap_z(value) for value in outer]
    middle = [swap_z(lax.optimization_barrier(both)[0]) for both in zip(middle, outer)]
    done = []
    for a, b, far, near in zip(keep, given, outer, middle):
        back = shift_row(added(a[2, 0], b[2, 0], jnp.where(first, zero, far)), -1)
        back = shift_row(added(a[1, 0], b[1, 0], near, back), -1)
        done.append(added(a[0, 0], b[0, 0], jnp.where(first, far, zero), back))
    return [added(half, swap_head(half)) for half in done]


def on_device(queries, key_rows, value_rows, d_out, seq_lengths):
    own = jnp.stack([key_rows, value_rows])
    row1 = shift_row(own, 1)
    side0 = swap_z(own, (0,))
    row2 = shift_row(row1, 1)
    side1 = swap_z(lax.optimization_barrier((row1, side0))[0])
    side2 = [swap_z(row2[part], (1,)) for part in range(2)]
    blocks = []
    for block in (own, side0, row1, side1, row2, *side2):
        blocks += [block, swap_core(block)]
    attended, grad_queries, *parts = attention(seq_lengths, queries, d_out, blocks)
    grad_keys, grad_values = returned(parts[::2], parts[1::2])
    return attended, grad_queries, grad_keys, grad_values


def solution(mesh):
    fine = Mesh(mesh.devices.reshape(4, 4, 2, 2, 2), ("x", "y", "zh", "core", "zl"))
    tokens = P("zl", SEQ, None)
    rows = P(SEQ, None)
    return jax.shard_map(
        on_device,
        mesh=fine,
        in_specs=(tokens, rows, rows, tokens, P()),
        out_specs=(tokens, tokens, rows, rows),
        check_vma=False,
    )
```
